32 devices in a mesh: row: 8 (over y, x, core), res: 4 (over z).
Axes of the slice: x: 2, y: 2, z: 4, core: 2. Of those that a mesh axis runs over, the one named last changes fastest.
Arguments:
- queries: bfloat16 [32, 256, 384], P('row', 'res'), may hold values from -64 to 64
- keys: bfloat16 [32, 256, 384], P('row', 'res'), may hold values from -4 to 4
- values: bfloat16 [32, 256, 384], P('row', 'res'), may hold values from -36 to 36
- out_weight: bfloat16 [384, 768], replicated, may hold values from -0.3125 to 0.3125
- grad_out: bfloat16 [32, 256, 768], P('row', 'res'), may hold values from -24 to 24
Outputs:
- mixed_out: bfloat16 [32, 256, 768], P('row', 'res')
- grad_query: bfloat16 [32, 256, 384], P('row', 'res')
- grad_key: bfloat16 [32, 256, 384], P('row', 'res')
- grad_value: bfloat16 [32, 256, 384], P('row', 'res')
The draws below stay inside these ranges and needn't reach their ends.
All inputs are finite; a program needn't handle non-finite values.
Results may differ from the reference program's by a relative error of at most 0.013.
Values may be sent and summed in bfloat16 or wider, within the bound.
A program may use at most 64 MiB of HBM per device.

```python
import math
import jax
import jax.numpy as jnp
from jax import lax

D = 768
HEADS = 6
HD = 64
SEQS = 32
L = 256
HH = 384


def base_keys(key):
    return jax.random.truncated_normal(key, -4.0, 4.0, (SEQS, L, HH), jnp.float32)


def draw_keys(key, part):
    field = base_keys(key)
    return field.astype(jnp.bfloat16)


def draw_queries(key, part):
    own_key = jax.random.fold_in(key, 23)
    field = jax.random.truncated_normal(own_key, -4.0, 4.0, (SEQS, L, HH), jnp.float32)
    return field.astype(jnp.bfloat16)


def levels(stream_key, dims, cuts, smallest, top_value):
    loudness = 1.0
    for position, shards_of in cuts:
        draws = jax.random.uniform(jax.random.fold_in(jax.random.fold_in(stream_key, 6), position), (shards_of,), jnp.float32, smallest / len(cuts), top_value / len(cuts))
        loudness = loudness * jnp.repeat(jnp.exp(draws), dims[position] // shards_of).reshape((-1,) + (1,) * (len(dims) - 1 - position))
    return loudness


def centred(rng, extent, spread, limit, split=(), held_as=jnp.bfloat16):
    values = jax.random.normal(rng, extent, jnp.float32) * spread
    if len(split) > 0:
        values = levels(rng, extent, split, -0.22, 0.18) * values
    return jnp.clip(values, min=-limit, max=limit).astype(held_as)


def setup_inputs(seed: int = 0) -> dict:
    streams_of = jax.random.split(jax.random.key(seed), 6)
    queries = draw_queries(jax.random.fold_in(streams_of[5], 71), 0)
    keys = draw_keys(jax.random.fold_in(streams_of[5], 71), 0)
    values = centred(streams_of[2], (SEQS, L, HH), 6.0, 36.0, ((0, 8), (1, 4)))
    out_weight = centred(streams_of[3], (HH, D), HH ** -0.5, 0.3125)
    grad_out = centred(streams_of[4], (SEQS, L, D), 4.0, 24.0, ((0, 8), (1, 4)))
    return dict(queries=queries, keys=keys, values=values, out_weight=out_weight, grad_out=grad_out)


def split_heads(array):
    return array.astype(jnp.float32).reshape(array.shape[0], array.shape[1], HEADS, HD)

def reference(queries, keys, values, out_weight, grad_out):
    logit_scale = 1.0 / math.sqrt(HD * SEQS)
    query_heads = split_heads(queries)
    key_heads = split_heads(keys)
    value_heads = split_heads(values)
    logits = jnp.einsum('sihd,sjhd->hij', query_heads, key_heads) * logit_scale
    top = lax.optimization_barrier(jnp.max(logits, axis=-1, keepdims=True))
    expo = jnp.exp(logits - top)
    weights = expo / lax.optimization_barrier(jnp.sum(expo, axis=-1, keepdims=True))
    weights16 = weights.astype(jnp.bfloat16)
    weights_wide = weights16.astype(jnp.float32)
    attended = jnp.einsum('hij,sjhd->sihd', weights_wide, value_heads).astype(jnp.bfloat16)
    mixed_out = jnp.dot(attended.reshape(SEQS * L, HH), out_weight, preferred_element_type=jnp.float32)
    mixed_out = mixed_out.astype(jnp.bfloat16).reshape(SEQS, L, D)
    grad_attended = lax.dot_general(grad_out.reshape(SEQS * L, D), out_weight, (((1,), (1,)), ((), ())), preferred_element_type=jnp.float32)
    grad_attended = grad_attended.astype(jnp.bfloat16).reshape(SEQS, L, HH)
    grad_heads = split_heads(grad_attended)
    grad_weights = jnp.einsum('sihd,sjhd->hij', grad_heads, value_heads)
    grad_scores = weights * (grad_weights - lax.optimization_barrier(jnp.sum(weights * grad_weights, axis=-1, keepdims=True)))
    grad_scores = grad_scores.astype(jnp.bfloat16).astype(jnp.float32)
    grad_query = (jnp.einsum('hij,sjhd->sihd', grad_scores, key_heads) * logit_scale).astype(jnp.bfloat16)
    grad_key = (jnp.einsum('hij,sihd->sjhd', grad_scores, query_heads) * logit_scale).astype(jnp.bfloat16)
    grad_value = jnp.einsum('hij,sihd->sjhd', weights_wide, grad_heads).astype(jnp.bfloat16)
    return (mixed_out, grad_query.reshape(SEQS, L, HH), grad_key.reshape(SEQS, L, HH), grad_value.reshape(SEQS, L, HH))
```

```python
import functools
import math

import jax
import jax.numpy as jnp
from jax import lax
from jax.experimental import pallas as pl
from jax.experimental.pallas import tpu as pltpu
from jax.sharding import PartitionSpec as P

HEADS = 6
MESH = pl.DeviceIdType.MESH
WHOLE_AT = (0, 4, 6, 10)
HALF_AT = (2, 3, 8, 9)
PIECES = ((0, True), (0, False), (1, False), (1, True), (2, True), (2, False), (3, False), (3, True))


def split_heads(array):
    return array.reshape(array.shape[0], array.shape[1], HEADS, array.shape[2] // HEADS)


def softmax_rows(logits):
    top = jnp.max(logits, axis=-1, keepdims=True)
    expo = jnp.exp(logits - top)
    return expo / jnp.sum(expo, axis=-1, keepdims=True)


def score_grad(weights, grads):
    return weights * (grads - jnp.sum(weights * grads, axis=-1, keepdims=True))


def on_device(queries, keys, values, out_weight, grad_out):
    seq_dev, res_dev, width = queries.shape
    model_dim = out_weight.shape[1]
    head_dim = width // HEADS
    total_res = res_dev * lax.axis_size("res")
    logit_scale = 1.0 / math.sqrt(head_dim * seq_dev * lax.axis_size("row"))
    grad_flat = lax.dot_general(
        grad_out.reshape(seq_dev * res_dev, model_dim),
        out_weight,
        (((1,), (1,)), ((), ())),
        preferred_element_type=jnp.float32,
    )
    grad_attended = grad_flat.astype(jnp.bfloat16).reshape(seq_dev, res_dev, width)
    key_all, value_all = (
        lax.all_gather(keys, "res", axis=1, tiled=True),
        lax.all_gather(values, "res", axis=1, tiled=True),
    )
    key_heads = split_heads(key_all)
    value_heads = split_heads(value_all)
    partial_logits = jnp.einsum(
        "sihd,sjhd->hij", split_heads(queries), key_heads, preferred_element_type=jnp.float32
    )
    partial_logits = partial_logits.reshape(HEADS * res_dev, total_res)
    tied_sum = lax.psum(partial_logits, "row") * logit_scale
    full_weights = softmax_rows(tied_sum)
    weights16 = full_weights.astype(jnp.bfloat16)
    weights_heads = weights16.reshape(HEADS, res_dev, total_res)
    attended = jnp.einsum(
        "hij,sjhd->sihd", weights_heads, value_heads, preferred_element_type=jnp.float32
    )
    attended = attended.astype(jnp.bfloat16).reshape(seq_dev * res_dev, width)
    mixed_out = jnp.dot(attended, out_weight, preferred_element_type=jnp.float32)
    mixed_out = mixed_out.astype(jnp.bfloat16).reshape(seq_dev, res_dev, model_dim)
    grad_partial = jnp.einsum(
        "sihd,sjhd->hij",
        split_heads(grad_attended),
        value_heads,
        preferred_element_type=jnp.float32,
    )
    grad_partial = grad_partial.reshape(HEADS * res_dev, total_res)
    tied_grads = lax.psum(grad_partial, "row")
    scores16 = score_grad(full_weights, tied_grads).astype(jnp.bfloat16)
    score_heads = scores16.reshape(HEADS, res_dev, total_res)
    grad_query = (
        jnp.einsum("hij,sjhd->sihd", score_heads, key_heads, preferred_element_type=jnp.float32)
        * logit_scale
    )
    grad_query = grad_query.astype(jnp.bfloat16).reshape(seq_dev, res_dev, width)
    query_all, grad_all = (
        lax.all_gather(queries, "res", axis=1, tiled=True),
        lax.all_gather(grad_attended, "res", axis=1, tiled=True),
    )
    weights_cols, scores_cols = (
        lax.all_to_all(weights_heads, "res", split_axis=2, concat_axis=1, tiled=True),
        lax.all_to_all(score_heads, "res", split_axis=2, concat_axis=1, tiled=True),
    )
    grad_value = jnp.einsum(
        "hij,sihd->sjhd", weights_cols, split_heads(grad_all), preferred_element_type=jnp.float32
    )
    grad_value = grad_value.astype(jnp.bfloat16).reshape(seq_dev, res_dev, width)
    grad_key = (
        jnp.einsum(
            "hij,sihd->sjhd",
            scores_cols,
            split_heads(query_all),
            preferred_element_type=jnp.float32,
        )
        * logit_scale
    )
    grad_key = grad_key.astype(jnp.bfloat16).reshape(seq_dev, res_dev, width)
    return (mixed_out, grad_query, grad_key, grad_value)


def dot_nt(a, b):
    return lax.dot_general(a, b, (((1,), (1,)), ((), ())), preferred_element_type=jnp.float32)


def dot_tn(a, b):
    return lax.dot_general(a, b, (((0,), (0,)), ((), ())), preferred_element_type=jnp.float32)


def dot_nn(a, b):
    return jnp.dot(a, b, preferred_element_type=jnp.float32)


def kernel(
    rows,
    scale,
    q_ref,
    k_ref,
    v_ref,
    w_ref,
    go_ref,
    mixed_ref,
    gq_ref,
    gk_ref,
    gv_ref,
    pack_in,
    held_in,
    pack_out,
    held_out,
    part,
    part_held,
    half_part,
    half_held,
    prob,
    zin_send,
    zin_recv,
    part_send,
    part_recv,
    half_send,
    half_recv,
    prob_send,
    prob_recv,
    zout_send,
    zout_recv,
):
    seqs, res, width = q_ref.shape
    total = 4 * res
    owned = total // rows
    hd = width // HEADS
    hh = hd // 2
    whole = seqs * hd
    me_r, me_z = lax.axis_index("row"), lax.axis_index("res")
    pair_z = me_z + 1 - 2 * lax.rem(me_z, 2)
    z_partners = (lax.rem(me_z + 2, 4), 3 - me_z, pair_z)
    r_partners = [lax.rem(me_r + d, rows) for d in range(1, rows)]
    pending = []

    barrier = pltpu.get_barrier_semaphore()
    for z in z_partners:
        pl.semaphore_signal(barrier, inc=1, device_id=(me_r, z), device_id_type=MESH)
    for r in r_partners:
        pl.semaphore_signal(barrier, inc=1, device_id=(r, me_z), device_id_type=MESH)

    def start(src, dst, send, recv, r, z):
        copy = pltpu.make_async_remote_copy(
            src_ref=src,
            dst_ref=dst,
            send_sem=send,
            recv_sem=recv,
            device_id=(r, z),
            device_id_type=MESH,
        )
        copy.start()
        pending.append(copy)
        return copy

    def pack(phase, array, x):
        for z in range(4):
            lo, lh = WHOLE_AT[z] * hh, HALF_AT[z] * hh
            pack_in[phase, array, z, :, :whole] = jnp.concatenate(
                [x[s][:, lo : lo + hd] for s in range(seqs)], axis=-1
            )
            pack_in[phase, array, z, :, whole:] = jnp.concatenate(
                [x[s][:, lh : lh + hh] for s in range(seqs)], axis=-1
            )

    def exchange(phase, sent, held, send_sem, recv_sem):
        copies = [
            start(
                sent.at[phase, :, z],
                held.at[phase, :, me_z],
                send_sem.at[phase, n],
                recv_sem.at[phase, n],
                me_r,
                z,
            )
            for n, z in enumerate(z_partners)
        ]
        held[phase, :, me_z] = sent[phase, :, me_z]
        return copies

    def gathered(phase, array):
        x = held_in[phase, array].reshape(total, width)
        return x[:, :whole], x[:, whole:]

    def spread_parts(phase, a, b):
        part[phase, 0] = dot_nt(a[0], b[0]).reshape(rows, owned, total)
        part[phase, 1] = dot_nt(a[1], b[1]).reshape(rows, owned, total)
        copies = [
            start(
                part.at[phase, :, r],
                part_held.at[phase, me_r],
                part_send.at[phase, n],
                part_recv.at[phase, n],
                r,
                me_z,
            )
            for n, r in enumerate(r_partners)
        ]
        part_held[phase, me_r] = part[phase, :, me_r]
        return copies

    def tied(phase, copies):
        for copy in copies:
            copy.wait_recv()
        half = part_held[phase, 0, 1]
        for r in range(1, rows):
            half = half + part_held[phase, r, 1]
        half_part[phase] = half
        copy = start(
            half_part.at[phase],
            half_held.at[phase],
            half_send.at[phase],
            half_recv.at[phase],
            me_r,
            pair_z,
        )
        full = part_held[phase, 0, 0]
        for r in range(1, rows):
            full = full + part_held[phase, r, 0]
        copy.wait_recv()
        return full, half + half_held[phase]

    def spread_probs(phase, values):
        for n in range(2):
            prob[phase, n, me_r] = values[n].astype(jnp.bfloat16)
        return [
            start(
                prob.at[phase, :, me_r],
                prob.at[phase, :, me_r],
                prob_send.at[phase, n],
                prob_recv.at[phase, n],
                r,
                me_z,
            )
            for n, r in enumerate(r_partners)
        ]

    def probs(phase, copies):
        for copy in copies:
            copy.wait_recv()
        return prob[phase, 0].reshape(total, total), prob[phase, 1].reshape(total, total)

    def emit(phase, array, full, half):
        pack_out[phase, array, :, :, :whole] = full.astype(jnp.bfloat16).reshape(4, res, whole)
        pack_out[phase, array, :, :, whole:] = half.astype(jnp.bfloat16).reshape(
            4, res, width - whole
        )

    def unpack(phase, array, s):
        pieces = []
        for z, is_whole in PIECES:
            at, size = (s * hd, hd) if is_whole else (whole + s * hh, hh)
            pieces.append(held_out[phase, array, z, :, at : at + size])
        return jnp.concatenate(pieces, axis=-1)

    pack(0, 0, [q_ref[s] for s in range(seqs)])
    pack(0, 1, [k_ref[s] for s in range(seqs)])
    pl.semaphore_wait(barrier, len(z_partners) + len(r_partners))
    first_in = exchange(0, pack_in, held_in, zin_send, zin_recv)
    pack(1, 0, [v_ref[s] for s in range(seqs)])
    ga = dot_nt(go_ref[...].reshape(seqs * res, go_ref.shape[2]), w_ref[...])
    ga = ga.astype(jnp.bfloat16)
    pack(1, 1, [ga[s * res : (s + 1) * res] for s in range(seqs)])
    second_in = exchange(1, pack_in, held_in, zin_send, zin_recv)

    for copy in first_in:
        copy.wait_recv()
    logit_parts = spread_parts(0, gathered(0, 0), gathered(0, 1))
    weights = [softmax_rows(x * scale) for x in tied(0, logit_parts)]
    weight_copies = spread_probs(0, weights)

    for copy in second_in:
        copy.wait_recv()
    grad_parts = spread_parts(1, gathered(1, 1), gathered(1, 0))

    w16 = probs(0, weight_copies)
    vals, grads = gathered(1, 0), gathered(1, 1)
    emit(0, 0, dot_nn(w16[0], vals[0]), dot_nn(w16[1], vals[1]))
    emit(0, 1, dot_tn(w16[0], grads[0]), dot_tn(w16[1], grads[1]))
    first_out = exchange(0, pack_out, held_out, zout_send, zout_recv)

    tied_grads = tied(1, grad_parts)
    scores = [score_grad(w, g) for w, g in zip(weights, tied_grads)]
    s16 = probs(1, spread_probs(1, scores))
    qs, ks = gathered(0, 0), gathered(0, 1)
    emit(1, 0, dot_nn(s16[0], ks[0]) * scale, dot_nn(s16[1], ks[1]) * scale)
    emit(1, 1, dot_tn(s16[0], qs[0]) * scale, dot_tn(s16[1], qs[1]) * scale)
    second_out = exchange(1, pack_out, held_out, zout_send, zout_recv)

    for copy in first_out:
        copy.wait_recv()
    for s in range(seqs):
        mixed_ref[s] = dot_nn(unpack(0, 0, s), w_ref[...]).astype(jnp.bfloat16)
        gv_ref[s] = unpack(0, 1, s)
    for copy in second_out:
        copy.wait_recv()
    for s in range(seqs):
        gq_ref[s] = unpack(1, 0, s)
        gk_ref[s] = unpack(1, 1, s)
    for copy in pending:
        copy.wait_send()


def fused(rows, queries, keys, values, out_weight, grad_out):
    seqs, res, width = queries.shape
    model_dim = out_weight.shape[1]
    total = 4 * res
    owned = total // rows
    scale = 1.0 / math.sqrt(width // HEADS * seqs * rows)
    bf16, f32 = jnp.bfloat16, jnp.float32
    dma = pltpu.SemaphoreType.DMA
    vmem = pl.BlockSpec(memory_space=pltpu.VMEM)
    same = jax.ShapeDtypeStruct(queries.shape, bf16)
    return pl.pallas_call(
        functools.partial(kernel, rows, scale),
        out_shape=(jax.ShapeDtypeStruct((seqs, res, model_dim), bf16), same, same, same),
        in_specs=[vmem] * 5,
        out_specs=(vmem,) * 4,
        scratch_shapes=[
            pltpu.VMEM((2, 2, 4, res, width), bf16),
            pltpu.VMEM((2, 2, 4, res, width), bf16),
            pltpu.VMEM((2, 2, 4, res, width), bf16),
            pltpu.VMEM((2, 2, 4, res, width), bf16),
            pltpu.VMEM((2, 2, rows, owned, total), f32),
            pltpu.VMEM((2, rows, 2, owned, total), f32),
            pltpu.VMEM((2, owned, total), f32),
            pltpu.VMEM((2, owned, total), f32),
            pltpu.VMEM((2, 2, rows, owned, total), bf16),
            dma((2, 3)),
            dma((2, 3)),
            dma((2, rows - 1)),
            dma((2, rows - 1)),
            dma((2,)),
            dma((2,)),
            dma((2, rows - 1)),
            dma((2, rows - 1)),
            dma((2, 3)),
            dma((2, 3)),
        ],
        compiler_params=pltpu.CompilerParams(
            collective_id=0, has_side_effects=True, vmem_limit_bytes=40 * 1024 * 1024
        ),
    )(queries, keys, values, out_weight, grad_out)


def fits(rows, cols, seqs, res, width):
    total = cols * res
    return (
        cols == 4
        and rows > 1
        and seqs == 4
        and width == HEADS * 64
        and res % 16 == 0
        and total % (16 * rows) == 0
        and total <= 512
    )


def solution(mesh):
    placed = (
        P("row", "res", None),
        P("row", "res", None),
        P("row", "res", None),
        P(),
        P("row", "res", None),
    )
    rows, cols = mesh.shape["row"], mesh.shape["res"]

    def body(queries, keys, values, out_weight, grad_out):
        if fits(rows, cols, *queries.shape):
            return fused(rows, queries, keys, values, out_weight, grad_out)
        return on_device(queries, keys, values, out_weight, grad_out)

    return jax.shard_map(
        body,
        mesh=mesh,
        in_specs=placed,
        out_specs=(
            P("row", "res", None),
            P("row", "res", None),
            P("row", "res", None),
            P("row", "res", None),
        ),
        check_vma=False,
    )
```

```python
import functools
import math

import jax
import jax.numpy as jnp
from jax import lax
from jax.experimental import pallas as pl
from jax.experimental.pallas import tpu as pltpu
from jax.sharding import PartitionSpec as P

HEADS = 6
MESH = pl.DeviceIdType.MESH
TILE = 128


def split_heads(array):
    return array.reshape(array.shape[0], array.shape[1], HEADS, array.shape[2] // HEADS)


def softmax_rows(logits):
    top = jnp.max(logits, axis=-1, keepdims=True)
    expo = jnp.exp(logits - top)
    return expo / jnp.sum(expo, axis=-1, keepdims=True)


def score_grad(weights, grads):
    return weights * (grads - jnp.sum(weights * grads, axis=-1, keepdims=True))


def on_device(queries, keys, values, out_weight, grad_out):
    seq_dev, res_dev, width = queries.shape
    model_dim = out_weight.shape[1]
    head_dim = width // HEADS
    total_res = res_dev * lax.axis_size("res")
    logit_scale = 1.0 / math.sqrt(head_dim * seq_dev * lax.axis_size("row"))
    grad_flat = lax.dot_general(
        grad_out.reshape(seq_dev * res_dev, model_dim),
        out_weight,
        (((1,), (1,)), ((), ())),
        preferred_element_type=jnp.float32,
    )
    grad_attended = grad_flat.astype(jnp.bfloat16).reshape(seq_dev, res_dev, width)
    key_all, value_all = (
        lax.all_gather(keys, "res", axis=1, tiled=True),
        lax.all_gather(values, "res", axis=1, tiled=True),
    )
    key_heads = split_heads(key_all)
    value_heads = split_heads(value_all)
    partial_logits = jnp.einsum(
        "sihd,sjhd->hij", split_heads(queries), key_heads, preferred_element_type=jnp.float32
    )
    partial_logits = partial_logits.reshape(HEADS * res_dev, total_res)
    tied_sum = lax.psum(partial_logits, "row") * logit_scale
    full_weights = softmax_rows(tied_sum)
    weights16 = full_weights.astype(jnp.bfloat16)
    weights_heads = weights16.reshape(HEADS, res_dev, total_res)
    attended = jnp.einsum(
        "hij,sjhd->sihd", weights_heads, value_heads, preferred_element_type=jnp.float32
    )
    attended = attended.astype(jnp.bfloat16).reshape(seq_dev * res_dev, width)
    mixed_out = jnp.dot(attended, out_weight, preferred_element_type=jnp.float32)
    mixed_out = mixed_out.astype(jnp.bfloat16).reshape(seq_dev, res_dev, model_dim)
    grad_partial = jnp.einsum(
        "sihd,sjhd->hij",
        split_heads(grad_attended),
        value_heads,
        preferred_element_type=jnp.float32,
    )
    grad_partial = grad_partial.reshape(HEADS * res_dev, total_res)
    tied_grads = lax.psum(grad_partial, "row")
    scores16 = score_grad(full_weights, tied_grads).astype(jnp.bfloat16)
    score_heads = scores16.reshape(HEADS, res_dev, total_res)
    grad_query = (
        jnp.einsum("hij,sjhd->sihd", score_heads, key_heads, preferred_element_type=jnp.float32)
        * logit_scale
    )
    grad_query = grad_query.astype(jnp.bfloat16).reshape(seq_dev, res_dev, width)
    query_all, grad_all = (
        lax.all_gather(queries, "res", axis=1, tiled=True),
        lax.all_gather(grad_attended, "res", axis=1, tiled=True),
    )
    weights_cols, scores_cols = (
        lax.all_to_all(weights_heads, "res", split_axis=2, concat_axis=1, tiled=True),
        lax.all_to_all(score_heads, "res", split_axis=2, concat_axis=1, tiled=True),
    )
    grad_value = jnp.einsum(
        "hij,sihd->sjhd", weights_cols, split_heads(grad_all), preferred_element_type=jnp.float32
    )
    grad_value = grad_value.astype(jnp.bfloat16).reshape(seq_dev, res_dev, width)
    grad_key = (
        jnp.einsum(
            "hij,sihd->sjhd",
            scores_cols,
            split_heads(query_all),
            preferred_element_type=jnp.float32,
        )
        * logit_scale
    )
    grad_key = grad_key.astype(jnp.bfloat16).reshape(seq_dev, res_dev, width)
    return (mixed_out, grad_query, grad_key, grad_value)


def dot_nt(a, b):
    return lax.dot_general(a, b, (((1,), (1,)), ((), ())), preferred_element_type=jnp.float32)


def dot_tn(a, b):
    return lax.dot_general(a, b, (((0,), (0,)), ((), ())), preferred_element_type=jnp.float32)


def dot_nn(a, b):
    return jnp.dot(a, b, preferred_element_type=jnp.float32)


def is_end(z):
    return z in (0, 3)


def tile_of(z):
    return pl.ds(0 if z == 0 else 2 * TILE, TILE)


def kernel(
    rows,
    scale,
    q_ref,
    k_ref,
    v_ref,
    w_hbm,
    go_hbm,
    mixed_ref,
    gq_ref,
    gk_ref,
    gv_ref,
    w_ref,
    go_ref,
    mid,
    ga_ref,
    packed,
    held,
    part,
    part_held,
    prob,
    sent_out,
    mid_held,
    att_ref,
    load_sem,
    zin_send,
    zin_recv,
    part_send,
    part_recv,
    prob_send,
    prob_recv,
    zout_send,
    zout_recv,
):
    me_r, me_z = lax.axis_index("row"), lax.axis_index("res")
    seqs, res, _ = q_ref.shape
    total = 4 * res
    owned = total // rows
    half = TILE // 2
    r_partners = [lax.rem(me_r + d, rows) for d in range(1, rows)]
    inputs = (q_ref, k_ref, v_ref)

    barrier = pltpu.get_barrier_semaphore()
    for d in range(1, 4):
        pl.semaphore_signal(
            barrier, inc=1, device_id=(me_r, lax.rem(me_z + d, 4)), device_id_type=MESH
        )
    for r in r_partners:
        pl.semaphore_signal(barrier, inc=1, device_id=(r, me_z), device_id_type=MESH)

    loads = [
        pltpu.make_async_copy(x.at[:, :, pl.ds(TILE, TILE)], mid.at[n], load_sem.at[n])
        for n, x in enumerate(inputs)
    ]
    loads.append(pltpu.make_async_copy(w_hbm, w_ref, load_sem.at[3]))
    loads.append(pltpu.make_async_copy(go_hbm, go_ref, load_sem.at[4]))
    for load in loads:
        load.start()
    pl.semaphore_wait(barrier, 3 + len(r_partners))

    def run(z):
        end = is_end(z)
        heads = 2 if end else 1
        blocks = seqs if end else seqs // 2
        partners = (z ^ 2, z ^ 3, z ^ 1)
        pending = []

        def start(src, dst, send, recv, device):
            copy = pltpu.make_async_remote_copy(
                src_ref=src,
                dst_ref=dst,
                send_sem=send,
                recv_sem=recv,
                device_id=device,
                device_id_type=MESH,
            )
            copy.start()
            pending.append(copy)

        def arrived(ref, sem):
            pltpu.make_async_copy(ref, ref, sem).wait()

        def slots(array, source):
            return held.at[array, source, pl.ds(0, blocks)]

        own = []
        if end:
            for n, x in enumerate(inputs):
                copy = pltpu.make_async_copy(x.at[:, :, tile_of(z)], slots(n, z), load_sem.at[5 + n])
                copy.start()
                own.append(copy)

        def send_in(array, x, to_ends):
            for n, p in enumerate(partners):
                if is_end(p) != to_ends:
                    continue
                if to_ends:
                    src, dst = x.at[:, :, tile_of(p)], held.at[array, z]
                else:
                    src, dst = packed.at[array, p - 1], held.at[array, z, pl.ds(0, seqs // 2)]
                start(src, dst, zin_send.at[array, n], zin_recv.at[array, n], (me_r, p))

        def pack(array, tiles):
            for s in range(seqs // 2):
                x, y = tiles[2 * s], tiles[2 * s + 1]
                packed[array, 0, s] = jnp.concatenate([x[:, :half], y[:, :half]], axis=-1)
                packed[array, 1, s] = jnp.concatenate([x[:, half:], y[:, half:]], axis=-1)
            if not end:
                held[array, z, : seqs // 2] = packed[array, z - 1]

        def input_of(array):
            if end:
                own_wait = own[array] if array < 3 else None
                if own_wait is not None:
                    own_wait.wait()
            for n, p in enumerate(partners):
                arrived(slots(array, p), zin_recv.at[array, n])

        def rows_of(array):
            return jnp.concatenate(
                [held[array, :, s].reshape(total, TILE) for s in range(blocks)], axis=-1
            )

        def first_head(x):
            return lax.rem(lax.broadcasted_iota(jnp.int32, x.shape, 1), TILE) < half

        def partial_sums(a, b):
            if not end:
                return [dot_nt(a, b)]
            first, zero = first_head(a), jnp.zeros_like(a)
            return [dot_nt(jnp.where(first, a, zero), b), dot_nt(jnp.where(first, zero, a), b)]

        def spread_parts(phase, sums):
            for h, x in enumerate(sums):
                part[phase, h] = x.reshape(rows, owned, total)
            for n, r in enumerate(r_partners):
                start(
                    part.at[phase, pl.ds(0, heads), r],
                    part_held.at[phase, me_r, pl.ds(0, heads)],
                    part_send.at[phase, n],
                    part_recv.at[phase, n],
                    (r, me_z),
                )
            for h in range(heads):
                part_held[phase, me_r, h] = part[phase, h, me_r]

        def tied(phase):
            for n in range(rows - 1):
                arrived(part_held.at[phase, n, pl.ds(0, heads)], part_recv.at[phase, n])
            sums = []
            for h in range(heads):
                x = part_held[phase, 0, h]
                for r in range(1, rows):
                    x = x + part_held[phase, r, h]
                sums.append(x)
            return sums

        def spread_probs(phase, values):
            for h, x in enumerate(values):
                prob[phase, h, me_r] = x.astype(jnp.bfloat16)
            for n, r in enumerate(r_partners):
                block = prob.at[phase, pl.ds(0, heads), me_r]
                start(block, block, prob_send.at[phase, n], prob_recv.at[phase, n], (r, me_z))

        def probs(phase):
            for n in range(rows - 1):
                arrived(prob.at[phase, pl.ds(0, heads), n], prob_recv.at[phase, n])
            return [prob[phase, h].reshape(total, total) for h in range(heads)]

        def emit(array, dot, weights, x, factor, out_ref):
            y = dot(weights[0], x)
            if end:
                y = jnp.where(first_head(y), y, dot(weights[1], x))
            if factor is not None:
                y = y * factor
            y = y.astype(jnp.bfloat16)
            for s in range(blocks):
                sent_out[array, :, s] = y[:, s * TILE : (s + 1) * TILE].reshape(4, res, TILE)
            for n, p in enumerate(partners):
                if end:
                    dst = out_ref.at[:, :, tile_of(z)]
                else:
                    dst = mid_held.at[array, z - 1]
                start(
                    sent_out.at[array, p, pl.ds(0, blocks)],
                    dst,
                    zout_send.at[array, n],
                    zout_recv.at[array, n],
                    (me_r, p),
                )
            if end:
                lo = 0 if z == 0 else 2 * TILE
                out_ref[:, :, lo : lo + TILE] = sent_out[array, z]
            else:
                mid_held[array, z - 1] = sent_out[array, z, : seqs // 2]

        def finish(array, out_ref):
            for n, p in enumerate(partners):
                if is_end(p):
                    arrived(out_ref.at[:, :, tile_of(p)], zout_recv.at[array, n])
                else:
                    arrived(mid_held.at[array, p - 1], zout_recv.at[array, n])
            for s in range(seqs // 2):
                x, y = mid_held[array, 0, s], mid_held[array, 1, s]
                out_ref[2 * s, :, TILE : 2 * TILE] = jnp.concatenate(
                    [x[:, :half], y[:, :half]], axis=-1
                )
                out_ref[2 * s + 1, :, TILE : 2 * TILE] = jnp.concatenate(
                    [x[:, half:], y[:, half:]], axis=-1
                )

        send_in(0, q_ref, True)
        send_in(1, k_ref, True)
        for n in range(2):
            loads[n].wait()
            pack(n, [mid[n, s] for s in range(seqs)])
            send_in(n, None, False)
        send_in(2, v_ref, True)
        loads[2].wait()
        pack(2, [mid[2, s] for s in range(seqs)])
        send_in(2, None, False)
        loads[3].wait()
        loads[4].wait()
        ga = dot_nt(go_ref[...].reshape(seqs * res, go_ref.shape[2]), w_ref[...])
        ga = ga.astype(jnp.bfloat16).reshape(seqs, res, 3 * TILE)
        ga_ref[...] = ga
        if end:
            lo = 0 if z == 0 else 2 * TILE
            held[3, z] = ga[:, :, lo : lo + TILE]
        pack(3, [ga[s, :, TILE : 2 * TILE] for s in range(seqs)])

        input_of(0)
        input_of(1)
        spread_parts(0, partial_sums(rows_of(0), rows_of(1)))
        send_in(3, ga_ref, True)
        send_in(3, None, False)
        weights = [softmax_rows(x * scale) for x in tied(0)]
        spread_probs(0, weights)

        input_of(2)
        input_of(3)
        vals, grads = rows_of(2), rows_of(3)
        spread_parts(1, partial_sums(grads, vals))

        w16 = probs(0)
        emit(0, dot_nn, w16, vals, None, att_ref)
        scores = [score_grad(w, g) for w, g in zip(weights, tied(1))]
        spread_probs(1, scores)
        emit(1, dot_tn, w16, grads, None, gv_ref)
        s16 = probs(1)
        emit(2, dot_nn, s16, rows_of(1), scale, gq_ref)
        emit(3, dot_tn, s16, rows_of(0), scale, gk_ref)

        finish(0, att_ref)
        mixed = dot_nn(att_ref[...].reshape(seqs * res, 3 * TILE), w_ref[...])
        mixed_ref[...] = mixed.astype(jnp.bfloat16).reshape(mixed_ref.shape)
        finish(1, gv_ref)
        finish(2, gq_ref)
        finish(3, gk_ref)
        for copy in pending:
            copy.wait_send()

    for z in range(4):
        pl.when(me_z == z)(functools.partial(run, z))


def fused(rows, queries, keys, values, out_weight, grad_out):
    seqs, res, width = queries.shape
    model_dim = out_weight.shape[1]
    total = 4 * res
    owned = total // rows
    scale = 1.0 / math.sqrt(width // HEADS * seqs * rows)
    bf16, f32 = jnp.bfloat16, jnp.float32
    dma = pltpu.SemaphoreType.DMA
    hbm = pl.BlockSpec(memory_space=pltpu.HBM)
    vmem = pl.BlockSpec(memory_space=pltpu.VMEM)
    same = jax.ShapeDtypeStruct(queries.shape, bf16)
    return pl.pallas_call(
        functools.partial(kernel, rows, scale),
        out_shape=(jax.ShapeDtypeStruct((seqs, res, model_dim), bf16), same, same, same),
        in_specs=[hbm] * 5,
        out_specs=(vmem,) * 4,
        scratch_shapes=[
            pltpu.VMEM(out_weight.shape, bf16),
            pltpu.VMEM(grad_out.shape, bf16),
            pltpu.VMEM((3, seqs, res, TILE), bf16),
            pltpu.VMEM((seqs, res, width), bf16),
            pltpu.VMEM((4, 2, seqs // 2, res, TILE), bf16),
            pltpu.VMEM((4, 4, seqs, res, TILE), bf16),
            pltpu.VMEM((2, 2, rows, owned, total), f32),
            pltpu.VMEM((2, rows, 2, owned, total), f32),
            pltpu.VMEM((2, 2, rows, owned, total), bf16),
            pltpu.VMEM((4, 4, seqs, res, TILE), bf16),
            pltpu.VMEM((4, 2, seqs // 2, res, TILE), bf16),
            pltpu.VMEM((seqs, res, width), bf16),
            dma((8,)),
            dma((4, 3)),
            dma((4, 3)),
            dma((2, rows - 1)),
            dma((2, rows - 1)),
            dma((2, rows - 1)),
            dma((2, rows - 1)),
            dma((4, 3)),
            dma((4, 3)),
        ],
        compiler_params=pltpu.CompilerParams(
            collective_id=0, has_side_effects=True, vmem_limit_bytes=62 * 1024 * 1024
        ),
    )(queries, keys, values, out_weight, grad_out)


def fits(rows, cols, seqs, res, width):
    total = cols * res
    return (
        cols == 4
        and rows > 1
        and seqs == 4
        and width == HEADS * 64
        and res % 16 == 0
        and total % (16 * rows) == 0
        and total <= 512
    )


def solution(mesh):
    placed = (
        P("row", "res", None),
        P("row", "res", None),
        P("row", "res", None),
        P(),
        P("row", "res", None),
    )
    rows, cols = mesh.shape["row"], mesh.shape["res"]

    def body(queries, keys, values, out_weight, grad_out):
        if fits(rows, cols, *queries.shape):
            return fused(rows, queries, keys, values, out_weight, grad_out)
        return on_device(queries, keys, values, out_weight, grad_out)

    return jax.shard_map(
        body,
        mesh=mesh,
        in_specs=placed,
        out_specs=(
            P("row", "res", None),
            P("row", "res", None),
            P("row", "res", None),
            P("row", "res", None),
        ),
        check_vma=False,
    )
```

```python
import functools
import math

import jax
import jax.numpy as jnp
from jax import lax
from jax.experimental import pallas as pl
from jax.experimental.pallas import tpu as pltpu
from jax.sharding import PartitionSpec as P

HEADS = 6
MESH = pl.DeviceIdType.MESH
TILE = 128


def split_heads(array):
    return array.reshape(array.shape[0], array.shape[1], HEADS, array.shape[2] // HEADS)


def softmax_rows(logits):
    top = jnp.max(logits, axis=-1, keepdims=True)
    expo = jnp.exp(logits - top)
    return expo / jnp.sum(expo, axis=-1, keepdims=True)


def score_grad(weights, grads):
    return weights * (grads - jnp.sum(weights * grads, axis=-1, keepdims=True))


def on_device(queries, keys, values, out_weight, grad_out):
    seq_dev, res_dev, width = queries.shape
    model_dim = out_weight.shape[1]
    head_dim = width // HEADS
    total_res = res_dev * lax.axis_size("res")
    logit_scale = 1.0 / math.sqrt(head_dim * seq_dev * lax.axis_size("row"))
    grad_flat = lax.dot_general(
        grad_out.reshape(seq_dev * res_dev, model_dim),
        out_weight,
        (((1,), (1,)), ((), ())),
        preferred_element_type=jnp.float32,
    )
    grad_attended = grad_flat.astype(jnp.bfloat16).reshape(seq_dev, res_dev, width)
    key_all, value_all = (
        lax.all_gather(keys, "res", axis=1, tiled=True),
        lax.all_gather(values, "res", axis=1, tiled=True),
    )
    key_heads = split_heads(key_all)
    value_heads = split_heads(value_all)
    partial_logits = jnp.einsum(
        "sihd,sjhd->hij", split_heads(queries), key_heads, preferred_element_type=jnp.float32
    )
    partial_logits = partial_logits.reshape(HEADS * res_dev, total_res)
    tied_sum = lax.psum(partial_logits, "row") * logit_scale
    full_weights = softmax_rows(tied_sum)
    weights16 = full_weights.astype(jnp.bfloat16)
    weights_heads = weights16.reshape(HEADS, res_dev, total_res)
    attended = jnp.einsum(
        "hij,sjhd->sihd", weights_heads, value_heads, preferred_element_type=jnp.float32
    )
    attended = attended.astype(jnp.bfloat16).reshape(seq_dev * res_dev, width)
    mixed_out = jnp.dot(attended, out_weight, preferred_element_type=jnp.float32)
    mixed_out = mixed_out.astype(jnp.bfloat16).reshape(seq_dev, res_dev, model_dim)
    grad_partial = jnp.einsum(
        "sihd,sjhd->hij",
        split_heads(grad_attended),
        value_heads,
        preferred_element_type=jnp.float32,
    )
    grad_partial = grad_partial.reshape(HEADS * res_dev, total_res)
    tied_grads = lax.psum(grad_partial, "row")
    scores16 = score_grad(full_weights, tied_grads).astype(jnp.bfloat16)
    score_heads = scores16.reshape(HEADS, res_dev, total_res)
    grad_query = (
        jnp.einsum("hij,sjhd->sihd", score_heads, key_heads, preferred_element_type=jnp.float32)
        * logit_scale
    )
    grad_query = grad_query.astype(jnp.bfloat16).reshape(seq_dev, res_dev, width)
    query_all, grad_all = (
        lax.all_gather(queries, "res", axis=1, tiled=True),
        lax.all_gather(grad_attended, "res", axis=1, tiled=True),
    )
    weights_cols, scores_cols = (
        lax.all_to_all(weights_heads, "res", split_axis=2, concat_axis=1, tiled=True),
        lax.all_to_all(score_heads, "res", split_axis=2, concat_axis=1, tiled=True),
    )
    grad_value = jnp.einsum(
        "hij,sihd->sjhd", weights_cols, split_heads(grad_all), preferred_element_type=jnp.float32
    )
    grad_value = grad_value.astype(jnp.bfloat16).reshape(seq_dev, res_dev, width)
    grad_key = (
        jnp.einsum(
            "hij,sihd->sjhd",
            scores_cols,
            split_heads(query_all),
            preferred_element_type=jnp.float32,
        )
        * logit_scale
    )
    grad_key = grad_key.astype(jnp.bfloat16).reshape(seq_dev, res_dev, width)
    return (mixed_out, grad_query, grad_key, grad_value)


def dot_nt(a, b):
    return lax.dot_general(a, b, (((1,), (1,)), ((), ())), preferred_element_type=jnp.float32)


def dot_tn(a, b):
    return lax.dot_general(a, b, (((0,), (0,)), ((), ())), preferred_element_type=jnp.float32)


def dot_nn(a, b):
    return jnp.dot(a, b, preferred_element_type=jnp.float32)


def is_end(z):
    return z in (0, 3)


def tile_of(z):
    return pl.ds(0 if z == 0 else 2 * TILE, TILE)


def kernel(
    rows,
    scale,
    q_ref,
    k_ref,
    v_ref,
    w_hbm,
    go_hbm,
    mixed_ref,
    gq_ref,
    gk_ref,
    gv_ref,
    w_ref,
    go_ref,
    mid,
    ga_ref,
    packed,
    held,
    part,
    pair_held,
    chip_part,
    part_held,
    prob,
    sent_out,
    mid_held,
    att_ref,
    load_sem,
    zin_send,
    zin_recv,
    pair_send,
    pair_recv,
    part_send,
    part_recv,
    prob_send,
    prob_recv,
    zout_send,
    zout_recv,
):
    me_r, me_z = lax.axis_index("row"), lax.axis_index("res")
    seqs, res, _ = q_ref.shape
    total = 4 * res
    owned = total // rows
    half = TILE // 2
    chips = rows // 2
    me_c, me_p = lax.rem(me_r, 2), me_r // 2
    sibling = me_r + 1 - 2 * me_c
    chip_ids = [lax.rem(me_p + d, chips) for d in range(1, chips)]
    inputs = (q_ref, k_ref, v_ref)

    barrier = pltpu.get_barrier_semaphore()
    for d in range(1, 4):
        pl.semaphore_signal(
            barrier, inc=1, device_id=(me_r, lax.rem(me_z + d, 4)), device_id_type=MESH
        )
    pl.semaphore_signal(barrier, inc=1, device_id=(sibling, me_z), device_id_type=MESH)
    for p in chip_ids:
        pl.semaphore_signal(barrier, inc=1, device_id=(2 * p + me_c, me_z), device_id_type=MESH)

    loads = [
        pltpu.make_async_copy(x.at[:, :, pl.ds(TILE, TILE)], mid.at[n], load_sem.at[n])
        for n, x in enumerate(inputs)
    ]
    loads.append(pltpu.make_async_copy(w_hbm, w_ref, load_sem.at[3]))
    loads.append(pltpu.make_async_copy(go_hbm, go_ref, load_sem.at[4]))
    for load in loads:
        load.start()
    pl.semaphore_wait(barrier, 4 + len(chip_ids))

    def run(z):
        end = is_end(z)
        heads = 2 if end else 1
        blocks = seqs if end else seqs // 2
        partners = (z ^ 2, z ^ 3, z ^ 1)
        pending = []

        def start(src, dst, send, recv, device):
            copy = pltpu.make_async_remote_copy(
                src_ref=src,
                dst_ref=dst,
                send_sem=send,
                recv_sem=recv,
                device_id=device,
                device_id_type=MESH,
            )
            copy.start()
            pending.append(copy)

        def arrived(ref, sem):
            pltpu.make_async_copy(ref, ref, sem).wait()

        def slots(array, source):
            return held.at[array, source, pl.ds(0, blocks)]

        own = []
        if end:
            for n, x in enumerate(inputs):
                copy = pltpu.make_async_copy(x.at[:, :, tile_of(z)], slots(n, z), load_sem.at[5 + n])
                copy.start()
                own.append(copy)

        def send_in(array, x, to_ends):
            for n, p in enumerate(partners):
                if is_end(p) != to_ends:
                    continue
                if to_ends:
                    src, dst = x.at[:, :, tile_of(p)], held.at[array, z]
                else:
                    src, dst = packed.at[array, p - 1], held.at[array, z, pl.ds(0, seqs // 2)]
                start(src, dst, zin_send.at[array, n], zin_recv.at[array, n], (me_r, p))

        def pack(array, tiles):
            for s in range(seqs // 2):
                x, y = tiles[2 * s], tiles[2 * s + 1]
                packed[array, 0, s] = jnp.concatenate([x[:, :half], y[:, :half]], axis=-1)
                packed[array, 1, s] = jnp.concatenate([x[:, half:], y[:, half:]], axis=-1)
            if not end:
                held[array, z, : seqs // 2] = packed[array, z - 1]

        def input_of(array):
            if end:
                own_wait = own[array] if array < 3 else None
                if own_wait is not None:
                    own_wait.wait()
            for n, p in enumerate(partners):
                arrived(slots(array, p), zin_recv.at[array, n])

        def rows_of(array):
            return jnp.concatenate(
                [held[array, :, s].reshape(total, TILE) for s in range(blocks)], axis=-1
            )

        def first_head(x):
            return lax.rem(lax.broadcasted_iota(jnp.int32, x.shape, 1), TILE) < half

        def partial_sums(a, b):
            if not end:
                return [dot_nt(a, b)]
            first, zero = first_head(a), jnp.zeros_like(a)
            return [dot_nt(jnp.where(first, a, zero), b), dot_nt(jnp.where(first, zero, a), b)]

        def pair_parts(phase, sums):
            for h, x in enumerate(sums):
                part[phase, h] = x.reshape(chips, 2, owned, total)
            start(
                part.at[phase, pl.ds(0, heads), :, 1 - me_c],
                pair_held.at[phase, pl.ds(0, heads)],
                pair_send.at[phase],
                pair_recv.at[phase],
                (sibling, me_z),
            )

        def chip_parts(phase):
            arrived(pair_held.at[phase, pl.ds(0, heads)], pair_recv.at[phase])
            for h in range(heads):
                chip_part[phase, h] = part[phase, h, :, me_c] + pair_held[phase, h]
            for n, p in enumerate(chip_ids):
                start(
                    chip_part.at[phase, pl.ds(0, heads), p],
                    part_held.at[phase, me_p, pl.ds(0, heads)],
                    part_send.at[phase, n],
                    part_recv.at[phase, n],
                    (2 * p + me_c, me_z),
                )
            for h in range(heads):
                part_held[phase, me_p, h] = chip_part[phase, h, me_p]

        def tied(phase):
            for n in range(chips - 1):
                arrived(part_held.at[phase, n, pl.ds(0, heads)], part_recv.at[phase, n])
            sums = []
            for h in range(heads):
                x = part_held[phase, 0, h]
                for p in range(1, chips):
                    x = x + part_held[phase, p, h]
                sums.append(x)
            return sums

        def send_prob(phase, n, r, device):
            block = prob.at[phase, pl.ds(0, heads), r]
            start(block, block, prob_send.at[phase, n], prob_recv.at[phase, n], (device, me_z))

        def spread_probs(phase, values):
            for h, x in enumerate(values):
                prob[phase, h, me_r] = x.astype(jnp.bfloat16)
            for n, p in enumerate(chip_ids):
                send_prob(phase, n, me_r, 2 * p + me_c)
            send_prob(phase, chips - 1, me_r, sibling)

        def forward_probs(phase):
            for n in range(chips - 1):
                r = 2 * lax.rem(me_p + chips - 1 - n, chips) + me_c
                arrived(prob.at[phase, pl.ds(0, heads), r], prob_recv.at[phase, n])
                send_prob(phase, chips + n, r, sibling)

        def probs(phase):
            for n in range(chips - 1, 2 * chips - 1):
                arrived(prob.at[phase, pl.ds(0, heads), 0], prob_recv.at[phase, n])
            return [prob[phase, h].reshape(total, total) for h in range(heads)]

        def product(array, dot, weights, x, factor):
            y = dot(weights[0], x)
            if end:
                y = jnp.where(first_head(y), y, dot(weights[1], x))
            if factor is not None:
                y = y * factor
            y = y.astype(jnp.bfloat16)
            for s in range(blocks):
                sent_out[array, :, s] = y[:, s * TILE : (s + 1) * TILE].reshape(4, res, TILE)

        def send_out(array, out_ref):
            for n, p in enumerate(partners):
                if end:
                    dst = out_ref.at[:, :, tile_of(z)]
                else:
                    dst = mid_held.at[array, z - 1]
                start(
                    sent_out.at[array, p, pl.ds(0, blocks)],
                    dst,
                    zout_send.at[array, n],
                    zout_recv.at[array, n],
                    (me_r, p),
                )
            if end:
                lo = 0 if z == 0 else 2 * TILE
                out_ref[:, :, lo : lo + TILE] = sent_out[array, z]
            else:
                mid_held[array, z - 1] = sent_out[array, z, : seqs // 2]

        def finish(array, out_ref):
            for n, p in enumerate(partners):
                if is_end(p):
                    arrived(out_ref.at[:, :, tile_of(p)], zout_recv.at[array, n])
                else:
                    arrived(mid_held.at[array, p - 1], zout_recv.at[array, n])
            for s in range(seqs // 2):
                x, y = mid_held[array, 0, s], mid_held[array, 1, s]
                out_ref[2 * s, :, TILE : 2 * TILE] = jnp.concatenate(
                    [x[:, :half], y[:, :half]], axis=-1
                )
                out_ref[2 * s + 1, :, TILE : 2 * TILE] = jnp.concatenate(
                    [x[:, half:], y[:, half:]], axis=-1
                )

        send_in(0, q_ref, True)
        send_in(1, k_ref, True)
        for n in range(2):
            loads[n].wait()
            pack(n, [mid[n, s] for s in range(seqs)])
            send_in(n, None, False)
        send_in(2, v_ref, True)
        loads[2].wait()
        pack(2, [mid[2, s] for s in range(seqs)])
        send_in(2, None, False)
        loads[3].wait()
        loads[4].wait()
        ga = dot_nt(go_ref[...].reshape(seqs * res, go_ref.shape[2]), w_ref[...])
        ga = ga.astype(jnp.bfloat16).reshape(seqs, res, 3 * TILE)
        ga_ref[...] = ga
        if end:
            lo = 0 if z == 0 else 2 * TILE
            held[3, z] = ga[:, :, lo : lo + TILE]
        pack(3, [ga[s, :, TILE : 2 * TILE] for s in range(seqs)])

        input_of(0)
        input_of(1)
        pair_parts(0, partial_sums(rows_of(0), rows_of(1)))
        chip_parts(0)
        send_in(3, ga_ref, True)
        send_in(3, None, False)
        weights = [softmax_rows(x * scale) for x in tied(0)]
        spread_probs(0, weights)
        forward_probs(0)

        input_of(2)
        input_of(3)
        vals, grads = rows_of(2), rows_of(3)
        pair_parts(1, partial_sums(grads, vals))
        w16 = probs(0)
        product(0, dot_nn, w16, vals, None)
        chip_parts(1)
        send_out(0, att_ref)
        product(1, dot_tn, w16, grads, None)
        scores = [score_grad(w, g) for w, g in zip(weights, tied(1))]
        spread_probs(1, scores)
        send_out(1, gv_ref)
        forward_probs(1)
        s16 = probs(1)
        product(2, dot_nn, s16, rows_of(1), scale)
        send_out(2, gq_ref)
        product(3, dot_tn, s16, rows_of(0), scale)
        send_out(3, gk_ref)

        finish(0, att_ref)
        mixed = dot_nn(att_ref[...].reshape(seqs * res, 3 * TILE), w_ref[...])
        mixed_ref[...] = mixed.astype(jnp.bfloat16).reshape(mixed_ref.shape)
        finish(1, gv_ref)
        finish(2, gq_ref)
        finish(3, gk_ref)
        for copy in pending:
            copy.wait_send()

    for z in range(4):
        pl.when(me_z == z)(functools.partial(run, z))


def copy_out(*refs):
    ins, outs, sem = refs[:4], refs[4:8], refs[8]
    copies = [pltpu.make_async_copy(x, y, sem.at[n]) for n, (x, y) in enumerate(zip(ins, outs))]
    for copy in copies:
        copy.start()
    for copy in copies:
        copy.wait()


def fused(rows, queries, keys, values, out_weight, grad_out):
    seqs, res, width = queries.shape
    model_dim = out_weight.shape[1]
    total = 4 * res
    owned = total // rows
    chips = rows // 2
    scale = 1.0 / math.sqrt(width // HEADS * seqs * rows)
    bf16, f32 = jnp.bfloat16, jnp.float32
    dma = pltpu.SemaphoreType.DMA
    hbm = pl.BlockSpec(memory_space=pltpu.HBM)
    vmem = pl.BlockSpec(memory_space=pltpu.VMEM)
    same = jax.ShapeDtypeStruct(queries.shape, bf16)
    shapes = (jax.ShapeDtypeStruct((seqs, res, model_dim), bf16), same, same, same)
    results = pl.pallas_call(
        functools.partial(kernel, rows, scale),
        out_shape=tuple(pltpu.VMEM(x.shape, x.dtype) for x in shapes),
        in_specs=[hbm] * 5,
        out_specs=(vmem,) * 4,
        scratch_shapes=[
            pltpu.VMEM(out_weight.shape, bf16),
            pltpu.VMEM(grad_out.shape, bf16),
            pltpu.VMEM((3, seqs, res, TILE), bf16),
            pltpu.VMEM((seqs, res, width), bf16),
            pltpu.VMEM((4, 2, seqs // 2, res, TILE), bf16),
            pltpu.VMEM((4, 4, seqs, res, TILE), bf16),
            pltpu.VMEM((2, 2, chips, 2, owned, total), f32),
            pltpu.VMEM((2, 2, chips, owned, total), f32),
            pltpu.VMEM((2, 2, chips, owned, total), f32),
            pltpu.VMEM((2, chips, 2, owned, total), f32),
            pltpu.VMEM((2, 2, rows, owned, total), bf16),
            pltpu.VMEM((4, 4, seqs, res, TILE), bf16),
            pltpu.VMEM((4, 2, seqs // 2, res, TILE), bf16),
            pltpu.VMEM((seqs, res, width), bf16),
            dma((8,)),
            dma((4, 3)),
            dma((4, 3)),
            dma((2,)),
            dma((2,)),
            dma((2, chips - 1)),
            dma((2, chips - 1)),
            dma((2, rows - 1)),
            dma((2, rows - 1)),
            dma((4, 3)),
            dma((4, 3)),
        ],
        compiler_params=pltpu.CompilerParams(
            collective_id=0, has_side_effects=True, vmem_limit_bytes=62 * 1024 * 1024
        ),
    )(queries, keys, values, out_weight, grad_out)
    return pl.pallas_call(
        copy_out,
        out_shape=shapes,
        in_specs=[pl.BlockSpec(memory_space=pl.ANY)] * 4,
        out_specs=(pl.BlockSpec(memory_space=pl.ANY),) * 4,
        scratch_shapes=[dma((4,))],
    )(*results)


def fits(rows, cols, seqs, res, width):
    total = cols * res
    return (
        cols == 4
        and rows > 1
        and rows % 2 == 0
        and seqs == 4
        and width == HEADS * 64
        and res % 16 == 0
        and total % (16 * rows) == 0
        and total <= 512
    )


def solution(mesh):
    placed = (
        P("row", "res", None),
        P("row", "res", None),
        P("row", "res", None),
        P(),
        P("row", "res", None),
    )
    rows, cols = mesh.shape["row"], mesh.shape["res"]

    def body(queries, keys, values, out_weight, grad_out):
        if fits(rows, cols, *queries.shape):
            return fused(rows, queries, keys, values, out_weight, grad_out)
        return on_device(queries, keys, values, out_weight, grad_out)

    return jax.shard_map(
        body,
        mesh=mesh,
        in_specs=placed,
        out_specs=(
            P("row", "res", None),
            P("row", "res", None),
            P("row", "res", None),
            P("row", "res", None),
        ),
        check_vma=False,
    )
```

```python
import functools
import math

import jax
import jax.numpy as jnp
from jax import lax
from jax.experimental import pallas as pl
from jax.experimental.pallas import tpu as pltpu
from jax.sharding import PartitionSpec as P

HEADS = 6
MESH = pl.DeviceIdType.MESH
TILE = 128


def split_heads(array):
    return array.reshape(array.shape[0], array.shape[1], HEADS, array.shape[2] // HEADS)


def softmax_rows(logits):
    top = jnp.max(logits, axis=-1, keepdims=True)
    expo = jnp.exp(logits - top)
    return expo / jnp.sum(expo, axis=-1, keepdims=True)


def score_grad(weights, grads):
    return weights * (grads - jnp.sum(weights * grads, axis=-1, keepdims=True))


def on_device(queries, keys, values, out_weight, grad_out):
    seq_dev, res_dev, width = queries.shape
    model_dim = out_weight.shape[1]
    head_dim = width // HEADS
    total_res = res_dev * lax.axis_size("res")
    logit_scale = 1.0 / math.sqrt(head_dim * seq_dev * lax.axis_size("row"))
    grad_flat = lax.dot_general(
        grad_out.reshape(seq_dev * res_dev, model_dim),
        out_weight,
        (((1,), (1,)), ((), ())),
        preferred_element_type=jnp.float32,
    )
    grad_attended = grad_flat.astype(jnp.bfloat16).reshape(seq_dev, res_dev, width)
    key_all, value_all = (
        lax.all_gather(keys, "res", axis=1, tiled=True),
        lax.all_gather(values, "res", axis=1, tiled=True),
    )
    key_heads = split_heads(key_all)
    value_heads = split_heads(value_all)
    partial_logits = jnp.einsum(
        "sihd,sjhd->hij", split_heads(queries), key_heads, preferred_element_type=jnp.float32
    )
    partial_logits = partial_logits.reshape(HEADS * res_dev, total_res)
    tied_sum = lax.psum(partial_logits, "row") * logit_scale
    full_weights = softmax_rows(tied_sum)
    weights16 = full_weights.astype(jnp.bfloat16)
    weights_heads = weights16.reshape(HEADS, res_dev, total_res)
    attended = jnp.einsum(
        "hij,sjhd->sihd", weights_heads, value_heads, preferred_element_type=jnp.float32
    )
    attended = attended.astype(jnp.bfloat16).reshape(seq_dev * res_dev, width)
    mixed_out = jnp.dot(attended, out_weight, preferred_element_type=jnp.float32)
    mixed_out = mixed_out.astype(jnp.bfloat16).reshape(seq_dev, res_dev, model_dim)
    grad_partial = jnp.einsum(
        "sihd,sjhd->hij",
        split_heads(grad_attended),
        value_heads,
        preferred_element_type=jnp.float32,
    )
    grad_partial = grad_partial.reshape(HEADS * res_dev, total_res)
    tied_grads = lax.psum(grad_partial, "row")
    scores16 = score_grad(full_weights, tied_grads).astype(jnp.bfloat16)
    score_heads = scores16.reshape(HEADS, res_dev, total_res)
    grad_query = (
        jnp.einsum("hij,sjhd->sihd", score_heads, key_heads, preferred_element_type=jnp.float32)
        * logit_scale
    )
    grad_query = grad_query.astype(jnp.bfloat16).reshape(seq_dev, res_dev, width)
    query_all, grad_all = (
        lax.all_gather(queries, "res", axis=1, tiled=True),
        lax.all_gather(grad_attended, "res", axis=1, tiled=True),
    )
    weights_cols, scores_cols = (
        lax.all_to_all(weights_heads, "res", split_axis=2, concat_axis=1, tiled=True),
        lax.all_to_all(score_heads, "res", split_axis=2, concat_axis=1, tiled=True),
    )
    grad_value = jnp.einsum(
        "hij,sihd->sjhd", weights_cols, split_heads(grad_all), preferred_element_type=jnp.float32
    )
    grad_value = grad_value.astype(jnp.bfloat16).reshape(seq_dev, res_dev, width)
    grad_key = (
        jnp.einsum(
            "hij,sihd->sjhd",
            scores_cols,
            split_heads(query_all),
            preferred_element_type=jnp.float32,
        )
        * logit_scale
    )
    grad_key = grad_key.astype(jnp.bfloat16).reshape(seq_dev, res_dev, width)
    return (mixed_out, grad_query, grad_key, grad_value)


def dot_nt(a, b):
    return lax.dot_general(a, b, (((1,), (1,)), ((), ())), preferred_element_type=jnp.float32)


def dot_tn(a, b):
    return lax.dot_general(a, b, (((0,), (0,)), ((), ())), preferred_element_type=jnp.float32)


def dot_nn(a, b):
    return jnp.dot(a, b, preferred_element_type=jnp.float32)


def is_end(z):
    return z in (0, 3)


def tile_of(z):
    return pl.ds(0 if z == 0 else 2 * TILE, TILE)


def kernel(
    rows,
    scale,
    q_ref,
    k_ref,
    v_ref,
    w_hbm,
    go_hbm,
    mixed_ref,
    gq_ref,
    gk_ref,
    gv_ref,
    w_ref,
    go_ref,
    mid,
    ga_ref,
    packed,
    held,
    part,
    pair_held,
    chip_part,
    part_held,
    prob,
    sent_out,
    mid_held,
    att_ref,
    load_sem,
    zin_send,
    zin_recv,
    pair_send,
    pair_recv,
    part_send,
    part_recv,
    prob_send,
    prob_recv,
    zout_send,
    zout_recv,
):
    me_r, me_z = lax.axis_index("row"), lax.axis_index("res")
    seqs, res, _ = q_ref.shape
    total = 4 * res
    owned = total // rows
    half = TILE // 2
    chips = rows // 2
    me_c, me_p = lax.rem(me_r, 2), me_r // 2
    sibling = me_r + 1 - 2 * me_c
    chip_ids = [lax.rem(me_p + d, chips) for d in range(1, chips)]
    inputs = (q_ref, k_ref, v_ref)

    barrier = pltpu.get_barrier_semaphore()
    for d in range(1, 4):
        pl.semaphore_signal(
            barrier, inc=1, device_id=(me_r, lax.rem(me_z + d, 4)), device_id_type=MESH
        )
    pl.semaphore_signal(barrier, inc=1, device_id=(sibling, me_z), device_id_type=MESH)
    for p in chip_ids:
        for c in range(2):
            pl.semaphore_signal(barrier, inc=1, device_id=(2 * p + c, me_z), device_id_type=MESH)

    loads = [
        pltpu.make_async_copy(x.at[:, :, pl.ds(TILE, TILE)], mid.at[n], load_sem.at[n])
        for n, x in enumerate(inputs)
    ]
    loads.append(pltpu.make_async_copy(w_hbm, w_ref, load_sem.at[3]))
    loads.append(pltpu.make_async_copy(go_hbm, go_ref, load_sem.at[4]))
    for load in loads:
        load.start()
    pl.semaphore_wait(barrier, 4 + 2 * len(chip_ids))

    def run(z):
        end = is_end(z)
        heads = 2 if end else 1
        blocks = seqs if end else seqs // 2
        partners = (z ^ 2, z ^ 3, z ^ 1)
        pending = []

        def start(src, dst, send, recv, device):
            copy = pltpu.make_async_remote_copy(
                src_ref=src,
                dst_ref=dst,
                send_sem=send,
                recv_sem=recv,
                device_id=device,
                device_id_type=MESH,
            )
            copy.start()
            pending.append(copy)

        def arrived(ref, sem):
            pltpu.make_async_copy(ref, ref, sem).wait()

        def slots(array, source):
            return held.at[array, source, pl.ds(0, blocks)]

        own = []
        if end:
            for n, x in enumerate(inputs):
                copy = pltpu.make_async_copy(x.at[:, :, tile_of(z)], slots(n, z), load_sem.at[5 + n])
                copy.start()
                own.append(copy)

        def send_in(array, x, to_ends):
            for n, p in enumerate(partners):
                if is_end(p) != to_ends:
                    continue
                if to_ends:
                    src, dst = x.at[:, :, tile_of(p)], held.at[array, z]
                else:
                    src, dst = packed.at[array, p - 1], held.at[array, z, pl.ds(0, seqs // 2)]
                start(src, dst, zin_send.at[array, n], zin_recv.at[array, n], (me_r, p))

        def pack(array, tiles):
            for s in range(seqs // 2):
                x, y = tiles[2 * s], tiles[2 * s + 1]
                packed[array, 0, s] = jnp.concatenate([x[:, :half], y[:, :half]], axis=-1)
                packed[array, 1, s] = jnp.concatenate([x[:, half:], y[:, half:]], axis=-1)
            if not end:
                held[array, z, : seqs // 2] = packed[array, z - 1]

        def input_of(array):
            if end:
                own_wait = own[array] if array < 3 else None
                if own_wait is not None:
                    own_wait.wait()
            for n, p in enumerate(partners):
                arrived(slots(array, p), zin_recv.at[array, n])

        def rows_of(array):
            return jnp.concatenate(
                [held[array, :, s].reshape(total, TILE) for s in range(blocks)], axis=-1
            )

        def first_head(x):
            return lax.rem(lax.broadcasted_iota(jnp.int32, x.shape, 1), TILE) < half

        def partial_sums(a, b):
            if not end:
                return [dot_nt(a, b)]
            first, zero = first_head(a), jnp.zeros_like(a)
            return [dot_nt(jnp.where(first, a, zero), b), dot_nt(jnp.where(first, zero, a), b)]

        def pair_parts(phase, sums):
            for h, x in enumerate(sums):
                part[phase, h] = x.reshape(chips, 2, owned, total)
            start(
                part.at[phase, pl.ds(0, heads), :, 1 - me_c],
                pair_held.at[phase, pl.ds(0, heads)],
                pair_send.at[phase],
                pair_recv.at[phase],
                (sibling, me_z),
            )

        def chip_parts(phase):
            arrived(pair_held.at[phase, pl.ds(0, heads)], pair_recv.at[phase])
            for h in range(heads):
                chip_part[phase, h] = part[phase, h, :, me_c] + pair_held[phase, h]
            for n, p in enumerate(chip_ids):
                start(
                    chip_part.at[phase, pl.ds(0, heads), p],
                    part_held.at[phase, me_p, pl.ds(0, heads)],
                    part_send.at[phase, n],
                    part_recv.at[phase, n],
                    (2 * p + me_c, me_z),
                )
            for h in range(heads):
                part_held[phase, me_p, h] = chip_part[phase, h, me_p]

        def tied(phase):
            for n in range(chips - 1):
                arrived(part_held.at[phase, n, pl.ds(0, heads)], part_recv.at[phase, n])
            sums = []
            for h in range(heads):
                x = part_held[phase, 0, h]
                for p in range(1, chips):
                    x = x + part_held[phase, p, h]
                sums.append(x)
            return sums

        def send_prob(phase, n, r, device):
            block = prob.at[phase, pl.ds(0, heads), r]
            start(block, block, prob_send.at[phase, n], prob_recv.at[phase, n], (device, me_z))

        def spread_probs(phase, values):
            for h, x in enumerate(values):
                prob[phase, h, me_r] = x.astype(jnp.bfloat16)
            for n, p in enumerate(chip_ids):
                send_prob(phase, n, me_r, 2 * p + me_c)
            send_prob(phase, chips - 1, me_r, sibling)
            if phase == 1:
                for n, p in enumerate(chip_ids):
                    send_prob(phase, chips + n, me_r, 2 * p + 1 - me_c)

        def forward_probs(phase):
            for n in range(chips - 1):
                r = 2 * lax.rem(me_p + chips - 1 - n, chips) + me_c
                arrived(prob.at[phase, pl.ds(0, heads), r], prob_recv.at[phase, n])
                send_prob(phase, chips + n, r, sibling)

        def probs(phase):
            for n in range(chips - 1 if phase == 0 else 0, 2 * chips - 1):
                arrived(prob.at[phase, pl.ds(0, heads), 0], prob_recv.at[phase, n])
            return [prob[phase, h].reshape(total, total) for h in range(heads)]

        def product(array, dot, weights, x, factor):
            y = dot(weights[0], x)
            if end:
                y = jnp.where(first_head(y), y, dot(weights[1], x))
            if factor is not None:
                y = y * factor
            y = y.astype(jnp.bfloat16)
            for s in range(blocks):
                sent_out[array, :, s] = y[:, s * TILE : (s + 1) * TILE].reshape(4, res, TILE)

        def send_out(array, out_ref):
            for n, p in enumerate(partners):
                if end:
                    dst = out_ref.at[:, :, tile_of(z)]
                else:
                    dst = mid_held.at[array, z - 1]
                start(
                    sent_out.at[array, p, pl.ds(0, blocks)],
                    dst,
                    zout_send.at[array, n],
                    zout_recv.at[array, n],
                    (me_r, p),
                )
            if end:
                lo = 0 if z == 0 else 2 * TILE
                out_ref[:, :, lo : lo + TILE] = sent_out[array, z]
            else:
                mid_held[array, z - 1] = sent_out[array, z, : seqs // 2]

        def finish(array, out_ref):
            for n, p in enumerate(partners):
                if is_end(p):
                    arrived(out_ref.at[:, :, tile_of(p)], zout_recv.at[array, n])
                else:
                    arrived(mid_held.at[array, p - 1], zout_recv.at[array, n])
            for s in range(seqs // 2):
                x, y = mid_held[array, 0, s], mid_held[array, 1, s]
                out_ref[2 * s, :, TILE : 2 * TILE] = jnp.concatenate(
                    [x[:, :half], y[:, :half]], axis=-1
                )
                out_ref[2 * s + 1, :, TILE : 2 * TILE] = jnp.concatenate(
                    [x[:, half:], y[:, half:]], axis=-1
                )

        send_in(0, q_ref, True)
        send_in(1, k_ref, True)
        for n in range(2):
            loads[n].wait()
            pack(n, [mid[n, s] for s in range(seqs)])
            send_in(n, None, False)
        send_in(2, v_ref, True)
        loads[2].wait()
        pack(2, [mid[2, s] for s in range(seqs)])
        send_in(2, None, False)
        loads[3].wait()
        loads[4].wait()
        ga = dot_nt(go_ref[...].reshape(seqs * res, go_ref.shape[2]), w_ref[...])
        ga = ga.astype(jnp.bfloat16).reshape(seqs, res, 3 * TILE)
        ga_ref[...] = ga
        if end:
            lo = 0 if z == 0 else 2 * TILE
            held[3, z] = ga[:, :, lo : lo + TILE]
        pack(3, [ga[s, :, TILE : 2 * TILE] for s in range(seqs)])

        input_of(0)
        input_of(1)
        pair_parts(0, partial_sums(rows_of(0), rows_of(1)))
        chip_parts(0)
        send_in(3, ga_ref, True)
        send_in(3, None, False)
        weights = [softmax_rows(x * scale) for x in tied(0)]
        spread_probs(0, weights)
        forward_probs(0)

        input_of(2)
        input_of(3)
        vals, grads = rows_of(2), rows_of(3)
        pair_parts(1, partial_sums(grads, vals))
        w16 = probs(0)
        product(0, dot_nn, w16, vals, None)
        chip_parts(1)
        send_out(0, att_ref)
        product(1, dot_tn, w16, grads, None)
        scores = [score_grad(w, g) for w, g in zip(weights, tied(1))]
        spread_probs(1, scores)
        send_out(1, gv_ref)
        s16 = probs(1)
        product(2, dot_nn, s16, rows_of(1), scale)
        send_out(2, gq_ref)
        product(3, dot_tn, s16, rows_of(0), scale)
        send_out(3, gk_ref)

        finish(0, att_ref)
        mixed = dot_nn(att_ref[...].reshape(seqs * res, 3 * TILE), w_ref[...])
        mixed_ref[...] = mixed.astype(jnp.bfloat16).reshape(mixed_ref.shape)
        finish(1, gv_ref)
        finish(2, gq_ref)
        finish(3, gk_ref)
        for copy in pending:
            copy.wait_send()

    for z in range(4):
        pl.when(me_z == z)(functools.partial(run, z))


def copy_out(*refs):
    ins, outs, sem = refs[:4], refs[4:8], refs[8]
    copies = [pltpu.make_async_copy(x, y, sem.at[n]) for n, (x, y) in enumerate(zip(ins, outs))]
    for copy in copies:
        copy.start()
    for copy in copies:
        copy.wait()


def fused(rows, queries, keys, values, out_weight, grad_out):
    seqs, res, width = queries.shape
    model_dim = out_weight.shape[1]
    total = 4 * res
    owned = total // rows
    chips = rows // 2
    scale = 1.0 / math.sqrt(width // HEADS * seqs * rows)
    bf16, f32 = jnp.bfloat16, jnp.float32
    dma = pltpu.SemaphoreType.DMA
    hbm = pl.BlockSpec(memory_space=pltpu.HBM)
    vmem = pl.BlockSpec(memory_space=pltpu.VMEM)
    same = jax.ShapeDtypeStruct(queries.shape, bf16)
    shapes = (jax.ShapeDtypeStruct((seqs, res, model_dim), bf16), same, same, same)
    results = pl.pallas_call(
        functools.partial(kernel, rows, scale),
        out_shape=tuple(pltpu.VMEM(x.shape, x.dtype) for x in shapes),
        in_specs=[hbm] * 5,
        out_specs=(vmem,) * 4,
        scratch_shapes=[
            pltpu.VMEM(out_weight.shape, bf16),
            pltpu.VMEM(grad_out.shape, bf16),
            pltpu.VMEM((3, seqs, res, TILE), bf16),
            pltpu.VMEM((seqs, res, width), bf16),
            pltpu.VMEM((4, 2, seqs // 2, res, TILE), bf16),
            pltpu.VMEM((4, 4, seqs, res, TILE), bf16),
            pltpu.VMEM((2, 2, chips, 2, owned, total), f32),
            pltpu.VMEM((2, 2, chips, owned, total), f32),
            pltpu.VMEM((2, 2, chips, owned, total), f32),
            pltpu.VMEM((2, chips, 2, owned, total), f32),
            pltpu.VMEM((2, 2, rows, owned, total), bf16),
            pltpu.VMEM((4, 4, seqs, res, TILE), bf16),
            pltpu.VMEM((4, 2, seqs // 2, res, TILE), bf16),
            pltpu.VMEM((seqs, res, width), bf16),
            dma((8,)),
            dma((4, 3)),
            dma((4, 3)),
            dma((2,)),
            dma((2,)),
            dma((2, chips - 1)),
            dma((2, chips - 1)),
            dma((2, rows - 1)),
            dma((2, rows - 1)),
            dma((4, 3)),
            dma((4, 3)),
        ],
        compiler_params=pltpu.CompilerParams(
            collective_id=0, has_side_effects=True, vmem_limit_bytes=62 * 1024 * 1024
        ),
    )(queries, keys, values, out_weight, grad_out)
    return pl.pallas_call(
        copy_out,
        out_shape=shapes,
        in_specs=[vmem] * 4,
        out_specs=(pl.BlockSpec(memory_space=pl.ANY),) * 4,
        scratch_shapes=[dma((4,))],
        compiler_params=pltpu.CompilerParams(vmem_limit_bytes=2 * 1024 * 1024),
    )(*results)


def fits(rows, cols, seqs, res, width):
    total = cols * res
    return (
        cols == 4
        and rows > 1
        and rows % 2 == 0
        and seqs == 4
        and width == HEADS * 64
        and res % 16 == 0
        and total % (16 * rows) == 0
        and total <= 512
    )


def solution(mesh):
    placed = (
        P("row", "res", None),
        P("row", "res", None),
        P("row", "res", None),
        P(),
        P("row", "res", None),
    )
    rows, cols = mesh.shape["row"], mesh.shape["res"]

    def body(queries, keys, values, out_weight, grad_out):
        if fits(rows, cols, *queries.shape):
            return fused(rows, queries, keys, values, out_weight, grad_out)
        return on_device(queries, keys, values, out_weight, grad_out)

    return jax.shard_map(
        body,
        mesh=mesh,
        in_specs=placed,
        out_specs=(
            P("row", "res", None),
            P("row", "res", None),
            P("row", "res", None),
            P("row", "res", None),
        ),
        check_vma=False,
    )
```

```python
import functools
import math

import jax
import jax.numpy as jnp
from jax import lax
from jax.experimental import pallas as pl
from jax.experimental.pallas import tpu as pltpu
from jax.sharding import PartitionSpec as P

HEADS = 6
MESH = pl.DeviceIdType.MESH
TILE = 128


def split_heads(array):
    return array.reshape(array.shape[0], array.shape[1], HEADS, array.shape[2] // HEADS)


def softmax_rows(logits):
    top = jnp.max(logits, axis=-1, keepdims=True)
    expo = jnp.exp(logits - top)
    return expo / jnp.sum(expo, axis=-1, keepdims=True)


def score_grad(weights, grads):
    return weights * (grads - jnp.sum(weights * grads, axis=-1, keepdims=True))


def on_device(queries, keys, values, out_weight, grad_out):
    seq_dev, res_dev, width = queries.shape
    model_dim = out_weight.shape[1]
    head_dim = width // HEADS
    total_res = res_dev * lax.axis_size("res")
    logit_scale = 1.0 / math.sqrt(head_dim * seq_dev * lax.axis_size("row"))
    grad_flat = lax.dot_general(
        grad_out.reshape(seq_dev * res_dev, model_dim),
        out_weight,
        (((1,), (1,)), ((), ())),
        preferred_element_type=jnp.float32,
    )
    grad_attended = grad_flat.astype(jnp.bfloat16).reshape(seq_dev, res_dev, width)
    key_all, value_all = (
        lax.all_gather(keys, "res", axis=1, tiled=True),
        lax.all_gather(values, "res", axis=1, tiled=True),
    )
    key_heads = split_heads(key_all)
    value_heads = split_heads(value_all)
    partial_logits = jnp.einsum(
        "sihd,sjhd->hij", split_heads(queries), key_heads, preferred_element_type=jnp.float32
    )
    partial_logits = partial_logits.reshape(HEADS * res_dev, total_res)
    tied_sum = lax.psum(partial_logits, "row") * logit_scale
    full_weights = softmax_rows(tied_sum)
    weights16 = full_weights.astype(jnp.bfloat16)
    weights_heads = weights16.reshape(HEADS, res_dev, total_res)
    attended = jnp.einsum(
        "hij,sjhd->sihd", weights_heads, value_heads, preferred_element_type=jnp.float32
    )
    attended = attended.astype(jnp.bfloat16).reshape(seq_dev * res_dev, width)
    mixed_out = jnp.dot(attended, out_weight, preferred_element_type=jnp.float32)
    mixed_out = mixed_out.astype(jnp.bfloat16).reshape(seq_dev, res_dev, model_dim)
    grad_partial = jnp.einsum(
        "sihd,sjhd->hij",
        split_heads(grad_attended),
        value_heads,
        preferred_element_type=jnp.float32,
    )
    grad_partial = grad_partial.reshape(HEADS * res_dev, total_res)
    tied_grads = lax.psum(grad_partial, "row")
    scores16 = score_grad(full_weights, tied_grads).astype(jnp.bfloat16)
    score_heads = scores16.reshape(HEADS, res_dev, total_res)
    grad_query = (
        jnp.einsum("hij,sjhd->sihd", score_heads, key_heads, preferred_element_type=jnp.float32)
        * logit_scale
    )
    grad_query = grad_query.astype(jnp.bfloat16).reshape(seq_dev, res_dev, width)
    query_all, grad_all = (
        lax.all_gather(queries, "res", axis=1, tiled=True),
        lax.all_gather(grad_attended, "res", axis=1, tiled=True),
    )
    weights_cols, scores_cols = (
        lax.all_to_all(weights_heads, "res", split_axis=2, concat_axis=1, tiled=True),
        lax.all_to_all(score_heads, "res", split_axis=2, concat_axis=1, tiled=True),
    )
    grad_value = jnp.einsum(
        "hij,sihd->sjhd", weights_cols, split_heads(grad_all), preferred_element_type=jnp.float32
    )
    grad_value = grad_value.astype(jnp.bfloat16).reshape(seq_dev, res_dev, width)
    grad_key = (
        jnp.einsum(
            "hij,sihd->sjhd",
            scores_cols,
            split_heads(query_all),
            preferred_element_type=jnp.float32,
        )
        * logit_scale
    )
    grad_key = grad_key.astype(jnp.bfloat16).reshape(seq_dev, res_dev, width)
    return (mixed_out, grad_query, grad_key, grad_value)


def dot_nt(a, b):
    return lax.dot_general(a, b, (((1,), (1,)), ((), ())), preferred_element_type=jnp.float32)


def dot_tn(a, b):
    return lax.dot_general(a, b, (((0,), (0,)), ((), ())), preferred_element_type=jnp.float32)


def dot_nn(a, b):
    return jnp.dot(a, b, preferred_element_type=jnp.float32)


def is_end(z):
    return z in (0, 3)


def tile_of(z):
    return pl.ds(0 if z == 0 else 2 * TILE, TILE)


def kernel(
    rows,
    scale,
    q_ref,
    k_ref,
    v_ref,
    w_hbm,
    go_hbm,
    mixed_ref,
    gq_ref,
    gk_ref,
    gv_ref,
    w_ref,
    go_ref,
    mid,
    ga_ref,
    packed,
    held,
    part,
    pair_held,
    chip_part,
    part_held,
    prob,
    sent_out,
    mid_held,
    att_ref,
    load_sem,
    zin_send,
    zin_recv,
    pair_send,
    pair_recv,
    part_send,
    part_recv,
    prob_send,
    prob_recv,
    zout_send,
    zout_recv,
):
    me_r, me_z = lax.axis_index("row"), lax.axis_index("res")
    seqs, res, _ = q_ref.shape
    total = 4 * res
    owned = total // rows
    half = TILE // 2
    chips = rows // 2
    me_c, me_p = lax.rem(me_r, 2), me_r // 2
    sibling = me_r + 1 - 2 * me_c
    chip_ids = [lax.rem(me_p + d, chips) for d in range(1, chips)]
    inputs = (q_ref, k_ref, v_ref)

    barrier = pltpu.get_barrier_semaphore()
    for d in range(1, 4):
        pl.semaphore_signal(
            barrier, inc=1, device_id=(me_r, lax.rem(me_z + d, 4)), device_id_type=MESH
        )
    pl.semaphore_signal(barrier, inc=1, device_id=(sibling, me_z), device_id_type=MESH)
    for p in chip_ids:
        pl.semaphore_signal(barrier, inc=1, device_id=(2 * p + me_c, me_z), device_id_type=MESH)

    loads = [
        pltpu.make_async_copy(x.at[:, :, pl.ds(TILE, TILE)], mid.at[n], load_sem.at[n])
        for n, x in enumerate(inputs)
    ]
    loads.append(pltpu.make_async_copy(w_hbm, w_ref, load_sem.at[3]))
    loads.append(pltpu.make_async_copy(go_hbm, go_ref, load_sem.at[4]))
    for load in loads:
        load.start()
    pl.semaphore_wait(barrier, 4 + len(chip_ids))

    def run(z):
        end = is_end(z)
        heads = 2 if end else 1
        blocks = seqs if end else seqs // 2
        partners = (z ^ 2, z ^ 3, z ^ 1)
        pending = []

        def start(src, dst, send, recv, device):
            copy = pltpu.make_async_remote_copy(
                src_ref=src,
                dst_ref=dst,
                send_sem=send,
                recv_sem=recv,
                device_id=device,
                device_id_type=MESH,
            )
            copy.start()
            pending.append(copy)

        def arrived(ref, sem):
            pltpu.make_async_copy(ref, ref, sem).wait()

        def slots(array, source):
            return held.at[array, source, pl.ds(0, blocks)]

        own = []
        if end:
            for n, x in enumerate(inputs):
                copy = pltpu.make_async_copy(x.at[:, :, tile_of(z)], slots(n, z), load_sem.at[5 + n])
                copy.start()
                own.append(copy)

        def send_in(array, x, to_ends):
            for n, p in enumerate(partners):
                if is_end(p) != to_ends:
                    continue
                if to_ends:
                    src, dst = x.at[:, :, tile_of(p)], held.at[array, z]
                else:
                    src, dst = packed.at[array, p - 1], held.at[array, z, pl.ds(0, seqs // 2)]
                start(src, dst, zin_send.at[array, n], zin_recv.at[array, n], (me_r, p))

        def pack(array, tiles):
            for s in range(seqs // 2):
                x, y = tiles[2 * s], tiles[2 * s + 1]
                packed[array, 0, s] = jnp.concatenate([x[:, :half], y[:, :half]], axis=-1)
                packed[array, 1, s] = jnp.concatenate([x[:, half:], y[:, half:]], axis=-1)
            if not end:
                held[array, z, : seqs // 2] = packed[array, z - 1]

        def input_of(array):
            if end:
                own_wait = own[array] if array < 3 else None
                if own_wait is not None:
                    own_wait.wait()
            for n, p in enumerate(partners):
                arrived(slots(array, p), zin_recv.at[array, n])

        def rows_of(array):
            return jnp.concatenate(
                [held[array, :, s].reshape(total, TILE) for s in range(blocks)], axis=-1
            )

        def first_head(x):
            return lax.rem(lax.broadcasted_iota(jnp.int32, x.shape, 1), TILE) < half

        def partial_sums(a, b):
            if not end:
                return [dot_nt(a, b)]
            first, zero = first_head(a), jnp.zeros_like(a)
            return [dot_nt(jnp.where(first, a, zero), b), dot_nt(jnp.where(first, zero, a), b)]

        def pair_parts(phase, sums):
            for h, x in enumerate(sums):
                part[phase, h] = x.reshape(chips, 2, owned, total)
            start(
                part.at[phase, pl.ds(0, heads), :, 1 - me_c],
                pair_held.at[phase, pl.ds(0, heads)],
                pair_send.at[phase],
                pair_recv.at[phase],
                (sibling, me_z),
            )

        def chip_parts(phase):
            arrived(pair_held.at[phase, pl.ds(0, heads)], pair_recv.at[phase])
            for h in range(heads):
                chip_part[phase, h] = part[phase, h, :, me_c] + pair_held[phase, h]
            for n, p in enumerate(chip_ids):
                start(
                    chip_part.at[phase, pl.ds(0, heads), p],
                    part_held.at[phase, me_p, pl.ds(0, heads)],
                    part_send.at[phase, n],
                    part_recv.at[phase, n],
                    (2 * p + me_c, me_z),
                )
            for h in range(heads):
                part_held[phase, me_p, h] = chip_part[phase, h, me_p]

        def tied(phase):
            for n in range(chips - 1):
                arrived(part_held.at[phase, n, pl.ds(0, heads)], part_recv.at[phase, n])
            sums = []
            for h in range(heads):
                x = part_held[phase, 0, h]
                for p in range(1, chips):
                    x = x + part_held[phase, p, h]
                sums.append(x)
            return sums

        def send_prob(phase, n, r, device):
            block = prob.at[phase, pl.ds(0, heads), r]
            start(block, block, prob_send.at[phase, n], prob_recv.at[phase, n], (device, me_z))

        def spread_probs(phase, values):
            for h, x in enumerate(values):
                prob[phase, h, me_r] = x.astype(jnp.bfloat16)
            for n, p in enumerate(chip_ids):
                send_prob(phase, n, me_r, 2 * p + me_c)
            send_prob(phase, chips - 1, me_r, sibling)

        def forward_probs(phase):
            for n in range(chips - 1):
                r = 2 * lax.rem(me_p + chips - 1 - n, chips) + me_c
                arrived(prob.at[phase, pl.ds(0, heads), r], prob_recv.at[phase, n])
                send_prob(phase, chips + n, r, sibling)

        def probs(phase):
            for n in range(chips - 1, 2 * chips - 1):
                arrived(prob.at[phase, pl.ds(0, heads), 0], prob_recv.at[phase, n])
            return [prob[phase, h].reshape(total, total) for h in range(heads)]

        def product(array, dot, weights, x, factor):
            y = dot(weights[0], x)
            if end:
                y = jnp.where(first_head(y), y, dot(weights[1], x))
            if factor is not None:
                y = y * factor
            y = y.astype(jnp.bfloat16)
            for s in range(blocks):
                sent_out[array, :, s] = y[:, s * TILE : (s + 1) * TILE].reshape(4, res, TILE)

        def send_out(array, out_ref):
            for n, p in enumerate(partners):
                if end:
                    dst = out_ref.at[:, :, tile_of(z)]
                else:
                    dst = mid_held.at[array, z - 1]
                start(
                    sent_out.at[array, p, pl.ds(0, blocks)],
                    dst,
                    zout_send.at[array, n],
                    zout_recv.at[array, n],
                    (me_r, p),
                )
            if end:
                lo = 0 if z == 0 else 2 * TILE
                out_ref[:, :, lo : lo + TILE] = sent_out[array, z]
            else:
                mid_held[array, z - 1] = sent_out[array, z, : seqs // 2]

        def finish(array, out_ref):
            for n, p in enumerate(partners):
                if is_end(p):
                    arrived(out_ref.at[:, :, tile_of(p)], zout_recv.at[array, n])
                else:
                    arrived(mid_held.at[array, p - 1], zout_recv.at[array, n])
            for s in range(seqs // 2):
                x, y = mid_held[array, 0, s], mid_held[array, 1, s]
                out_ref[2 * s, :, TILE : 2 * TILE] = jnp.concatenate(
                    [x[:, :half], y[:, :half]], axis=-1
                )
                out_ref[2 * s + 1, :, TILE : 2 * TILE] = jnp.concatenate(
                    [x[:, half:], y[:, half:]], axis=-1
                )

        send_in(0, q_ref, True)
        send_in(1, k_ref, True)
        for n in range(2):
            loads[n].wait()
            pack(n, [mid[n, s] for s in range(seqs)])
            send_in(n, None, False)
        loads[2].wait()
        pack(2, [mid[2, s] for s in range(seqs)])
        loads[3].wait()
        loads[4].wait()
        ga = dot_nt(go_ref[...].reshape(seqs * res, go_ref.shape[2]), w_ref[...])
        ga = ga.astype(jnp.bfloat16).reshape(seqs, res, 3 * TILE)
        ga_ref[...] = ga
        if end:
            lo = 0 if z == 0 else 2 * TILE
            held[3, z] = ga[:, :, lo : lo + TILE]
        pack(3, [ga[s, :, TILE : 2 * TILE] for s in range(seqs)])

        while pending:
            pending.pop(0).wait_send()
        send_in(2, v_ref, True)
        send_in(2, None, False)
        input_of(0)
        input_of(1)
        pair_parts(0, partial_sums(rows_of(0), rows_of(1)))
        chip_parts(0)
        send_in(3, ga_ref, True)
        send_in(3, None, False)
        weights = [softmax_rows(x * scale) for x in tied(0)]
        spread_probs(0, weights)
        forward_probs(0)

        input_of(2)
        input_of(3)
        vals, grads = rows_of(2), rows_of(3)
        pair_parts(1, partial_sums(grads, vals))
        w16 = probs(0)
        product(0, dot_nn, w16, vals, None)
        send_out(0, att_ref)
        chip_parts(1)
        product(1, dot_tn, w16, grads, None)
        send_out(1, gv_ref)
        scores = [score_grad(w, g) for w, g in zip(weights, tied(1))]
        spread_probs(1, scores)
        forward_probs(1)
        s16 = probs(1)
        product(2, dot_nn, s16, rows_of(1), scale)
        send_out(2, gq_ref)
        product(3, dot_tn, s16, rows_of(0), scale)
        send_out(3, gk_ref)

        finish(0, att_ref)
        mixed = dot_nn(att_ref[...].reshape(seqs * res, 3 * TILE), w_ref[...])
        mixed_ref[...] = mixed.astype(jnp.bfloat16).reshape(mixed_ref.shape)
        finish(1, gv_ref)
        finish(2, gq_ref)
        finish(3, gk_ref)
        for copy in pending:
            copy.wait_send()

    for z in range(4):
        pl.when(me_z == z)(functools.partial(run, z))


def copy_out(*refs):
    ins, outs, sem = refs[:4], refs[4:8], refs[8]
    copies = [pltpu.make_async_copy(x, y, sem.at[n]) for n, (x, y) in enumerate(zip(ins, outs))]
    for copy in copies:
        copy.start()
    for copy in copies:
        copy.wait()


def fused(rows, queries, keys, values, out_weight, grad_out):
    seqs, res, width = queries.shape
    model_dim = out_weight.shape[1]
    total = 4 * res
    owned = total // rows
    chips = rows // 2
    scale = 1.0 / math.sqrt(width // HEADS * seqs * rows)
    bf16, f32 = jnp.bfloat16, jnp.float32
    dma = pltpu.SemaphoreType.DMA
    hbm = pl.BlockSpec(memory_space=pltpu.HBM)
    vmem = pl.BlockSpec(memory_space=pltpu.VMEM)
    same = jax.ShapeDtypeStruct(queries.shape, bf16)
    shapes = (jax.ShapeDtypeStruct((seqs, res, model_dim), bf16), same, same, same)
    results = pl.pallas_call(
        functools.partial(kernel, rows, scale),
        out_shape=tuple(pltpu.VMEM(x.shape, x.dtype) for x in shapes),
        in_specs=[hbm] * 5,
        out_specs=(vmem,) * 4,
        scratch_shapes=[
            pltpu.VMEM(out_weight.shape, bf16),
            pltpu.VMEM(grad_out.shape, bf16),
            pltpu.VMEM((3, seqs, res, TILE), bf16),
            pltpu.VMEM((seqs, res, width), bf16),
            pltpu.VMEM((4, 2, seqs // 2, res, TILE), bf16),
            pltpu.VMEM((4, 4, seqs, res, TILE), bf16),
            pltpu.VMEM((2, 2, chips, 2, owned, total), f32),
            pltpu.VMEM((2, 2, chips, owned, total), f32),
            pltpu.VMEM((2, 2, chips, owned, total), f32),
            pltpu.VMEM((2, chips, 2, owned, total), f32),
            pltpu.VMEM((2, 2, rows, owned, total), bf16),
            pltpu.VMEM((4, 4, seqs, res, TILE), bf16),
            pltpu.VMEM((4, 2, seqs // 2, res, TILE), bf16),
            pltpu.VMEM((seqs, res, width), bf16),
            dma((8,)),
            dma((4, 3)),
            dma((4, 3)),
            dma((2,)),
            dma((2,)),
            dma((2, chips - 1)),
            dma((2, chips - 1)),
            dma((2, rows - 1)),
            dma((2, rows - 1)),
            dma((4, 3)),
            dma((4, 3)),
        ],
        compiler_params=pltpu.CompilerParams(
            collective_id=0, has_side_effects=True, vmem_limit_bytes=62 * 1024 * 1024
        ),
    )(queries, keys, values, out_weight, grad_out)
    return pl.pallas_call(
        copy_out,
        out_shape=shapes,
        in_specs=[vmem] * 4,
        out_specs=(pl.BlockSpec(memory_space=pl.ANY),) * 4,
        scratch_shapes=[dma((4,))],
        compiler_params=pltpu.CompilerParams(vmem_limit_bytes=2 * 1024 * 1024),
    )(*results)


def fits(rows, cols, seqs, res, width):
    total = cols * res
    return (
        cols == 4
        and rows > 1
        and rows % 2 == 0
        and seqs == 4
        and width == HEADS * 64
        and res % 16 == 0
        and total % (16 * rows) == 0
        and total <= 512
    )


def solution(mesh):
    placed = (
        P("row", "res", None),
        P("row", "res", None),
        P("row", "res", None),
        P(),
        P("row", "res", None),
    )
    rows, cols = mesh.shape["row"], mesh.shape["res"]

    def body(queries, keys, values, out_weight, grad_out):
        if fits(rows, cols, *queries.shape):
            return fused(rows, queries, keys, values, out_weight, grad_out)
        return on_device(queries, keys, values, out_weight, grad_out)

    return jax.shard_map(
        body,
        mesh=mesh,
        in_specs=placed,
        out_specs=(
            P("row", "res", None),
            P("row", "res", None),
            P("row", "res", None),
            P("row", "res", None),
        ),
        check_vma=False,
    )
```

```python
import functools
import math

import jax
import jax.numpy as jnp
from jax import lax
from jax.experimental import pallas as pl
from jax.experimental.pallas import tpu as pltpu
from jax.sharding import PartitionSpec as P

HEADS = 6
MESH = pl.DeviceIdType.MESH
TILE = 128


def split_heads(array):
    return array.reshape(array.shape[0], array.shape[1], HEADS, array.shape[2] // HEADS)


def softmax_rows(logits):
    top = jnp.max(logits, axis=-1, keepdims=True)
    expo = jnp.exp(logits - top)
    return expo / jnp.sum(expo, axis=-1, keepdims=True)


def score_grad(weights, grads):
    return weights * (grads - jnp.sum(weights * grads, axis=-1, keepdims=True))


def on_device(queries, keys, values, out_weight, grad_out):
    seq_dev, res_dev, width = queries.shape
    model_dim = out_weight.shape[1]
    head_dim = width // HEADS
    total_res = res_dev * lax.axis_size("res")
    logit_scale = 1.0 / math.sqrt(head_dim * seq_dev * lax.axis_size("row"))
    grad_flat = lax.dot_general(
        grad_out.reshape(seq_dev * res_dev, model_dim),
        out_weight,
        (((1,), (1,)), ((), ())),
        preferred_element_type=jnp.float32,
    )
    grad_attended = grad_flat.astype(jnp.bfloat16).reshape(seq_dev, res_dev, width)
    key_all, value_all = (
        lax.all_gather(keys, "res", axis=1, tiled=True),
        lax.all_gather(values, "res", axis=1, tiled=True),
    )
    key_heads = split_heads(key_all)
    value_heads = split_heads(value_all)
    partial_logits = jnp.einsum(
        "sihd,sjhd->hij", split_heads(queries), key_heads, preferred_element_type=jnp.float32
    )
    partial_logits = partial_logits.reshape(HEADS * res_dev, total_res)
    tied_sum = lax.psum(partial_logits, "row") * logit_scale
    full_weights = softmax_rows(tied_sum)
    weights16 = full_weights.astype(jnp.bfloat16)
    weights_heads = weights16.reshape(HEADS, res_dev, total_res)
    attended = jnp.einsum(
        "hij,sjhd->sihd", weights_heads, value_heads, preferred_element_type=jnp.float32
    )
    attended = attended.astype(jnp.bfloat16).reshape(seq_dev * res_dev, width)
    mixed_out = jnp.dot(attended, out_weight, preferred_element_type=jnp.float32)
    mixed_out = mixed_out.astype(jnp.bfloat16).reshape(seq_dev, res_dev, model_dim)
    grad_partial = jnp.einsum(
        "sihd,sjhd->hij",
        split_heads(grad_attended),
        value_heads,
        preferred_element_type=jnp.float32,
    )
    grad_partial = grad_partial.reshape(HEADS * res_dev, total_res)
    tied_grads = lax.psum(grad_partial, "row")
    scores16 = score_grad(full_weights, tied_grads).astype(jnp.bfloat16)
    score_heads = scores16.reshape(HEADS, res_dev, total_res)
    grad_query = (
        jnp.einsum("hij,sjhd->sihd", score_heads, key_heads, preferred_element_type=jnp.float32)
        * logit_scale
    )
    grad_query = grad_query.astype(jnp.bfloat16).reshape(seq_dev, res_dev, width)
    query_all, grad_all = (
        lax.all_gather(queries, "res", axis=1, tiled=True),
        lax.all_gather(grad_attended, "res", axis=1, tiled=True),
    )
    weights_cols, scores_cols = (
        lax.all_to_all(weights_heads, "res", split_axis=2, concat_axis=1, tiled=True),
        lax.all_to_all(score_heads, "res", split_axis=2, concat_axis=1, tiled=True),
    )
    grad_value = jnp.einsum(
        "hij,sihd->sjhd", weights_cols, split_heads(grad_all), preferred_element_type=jnp.float32
    )
    grad_value = grad_value.astype(jnp.bfloat16).reshape(seq_dev, res_dev, width)
    grad_key = (
        jnp.einsum(
            "hij,sihd->sjhd",
            scores_cols,
            split_heads(query_all),
            preferred_element_type=jnp.float32,
        )
        * logit_scale
    )
    grad_key = grad_key.astype(jnp.bfloat16).reshape(seq_dev, res_dev, width)
    return (mixed_out, grad_query, grad_key, grad_value)


def dot_nt(a, b):
    return lax.dot_general(a, b, (((1,), (1,)), ((), ())), preferred_element_type=jnp.float32)


def dot_tn(a, b):
    return lax.dot_general(a, b, (((0,), (0,)), ((), ())), preferred_element_type=jnp.float32)


def dot_nn(a, b):
    return jnp.dot(a, b, preferred_element_type=jnp.float32)


def is_end(z):
    return z in (0, 3)


def tile_of(z):
    return pl.ds(0 if z == 0 else 2 * TILE, TILE)


def kernel(
    rows,
    scale,
    q_ref,
    k_ref,
    v_ref,
    w_hbm,
    go_hbm,
    mixed_ref,
    gq_ref,
    gk_ref,
    gv_ref,
    w_ref,
    go_ref,
    mid,
    ga_ref,
    packed,
    held,
    part,
    pair_held,
    chip_part,
    part_held,
    prob,
    sent_out,
    mid_held,
    att_ref,
    load_sem,
    zin_send,
    zin_recv,
    pair_send,
    pair_recv,
    part_send,
    part_recv,
    prob_send,
    prob_recv,
    zout_send,
    zout_recv,
):
    me_r, me_z = lax.axis_index("row"), lax.axis_index("res")
    seqs, res, _ = q_ref.shape
    total = 4 * res
    owned = total // rows
    half = TILE // 2
    chips = rows // 2
    me_c, me_p = lax.rem(me_r, 2), me_r // 2
    sibling = me_r + 1 - 2 * me_c
    chip_ids = [lax.rem(me_p + d, chips) for d in range(1, chips)]
    inputs = (q_ref, k_ref, v_ref)

    barrier = pltpu.get_barrier_semaphore()
    for d in range(1, 4):
        pl.semaphore_signal(
            barrier, inc=1, device_id=(me_r, lax.rem(me_z + d, 4)), device_id_type=MESH
        )
    pl.semaphore_signal(barrier, inc=1, device_id=(sibling, me_z), device_id_type=MESH)
    for p in chip_ids:
        pl.semaphore_signal(barrier, inc=1, device_id=(2 * p + me_c, me_z), device_id_type=MESH)

    loads = [
        pltpu.make_async_copy(x.at[:, :, pl.ds(TILE, TILE)], mid.at[n], load_sem.at[n])
        for n, x in enumerate(inputs)
    ]
    loads.append(pltpu.make_async_copy(w_hbm, w_ref, load_sem.at[3]))
    loads.append(pltpu.make_async_copy(go_hbm, go_ref, load_sem.at[4]))
    for load in loads:
        load.start()
    pl.semaphore_wait(barrier, 4 + len(chip_ids))

    def run(z):
        end = is_end(z)
        heads = 2 if end else 1
        blocks = seqs if end else seqs // 2
        partners = (z ^ 2, z ^ 3, z ^ 1)
        pending = []

        def start(src, dst, send, recv, device):
            copy = pltpu.make_async_remote_copy(
                src_ref=src,
                dst_ref=dst,
                send_sem=send,
                recv_sem=recv,
                device_id=device,
                device_id_type=MESH,
            )
            copy.start()
            pending.append(copy)

        def arrived(ref, sem):
            pltpu.make_async_copy(ref, ref, sem).wait()

        def slots(array, source):
            return held.at[array, source, pl.ds(0, blocks)]

        own = []
        if end:
            for n, x in enumerate(inputs):
                copy = pltpu.make_async_copy(x.at[:, :, tile_of(z)], slots(n, z), load_sem.at[5 + n])
                copy.start()
                own.append(copy)

        def send_in(array, x, to_ends):
            for n, p in enumerate(partners):
                if is_end(p) != to_ends:
                    continue
                if to_ends:
                    src, dst = x.at[:, :, tile_of(p)], held.at[array, z]
                else:
                    src, dst = packed.at[array, p - 1], held.at[array, z, pl.ds(0, seqs // 2)]
                start(src, dst, zin_send.at[array, n], zin_recv.at[array, n], (me_r, p))

        def pack(array, tiles):
            for s in range(seqs // 2):
                x, y = tiles[2 * s], tiles[2 * s + 1]
                packed[array, 0, s] = jnp.concatenate([x[:, :half], y[:, :half]], axis=-1)
                packed[array, 1, s] = jnp.concatenate([x[:, half:], y[:, half:]], axis=-1)
            if not end:
                held[array, z, : seqs // 2] = packed[array, z - 1]

        def input_of(array):
            if end:
                own_wait = own[array] if array < 3 else None
                if own_wait is not None:
                    own_wait.wait()
            for n, p in enumerate(partners):
                arrived(slots(array, p), zin_recv.at[array, n])

        def rows_of(array):
            return jnp.concatenate(
                [held[array, :, s].reshape(total, TILE) for s in range(blocks)], axis=-1
            )

        def first_head(x):
            return lax.rem(lax.broadcasted_iota(jnp.int32, x.shape, 1), TILE) < half

        def partial_sums(a, b):
            if not end:
                return [dot_nt(a, b)]
            first, zero = first_head(a), jnp.zeros_like(a)
            return [dot_nt(jnp.where(first, a, zero), b), dot_nt(jnp.where(first, zero, a), b)]

        def pair_parts(phase, sums):
            for h, x in enumerate(sums):
                part[phase, h] = x.reshape(chips, 2, owned, total)
                start(
                    part.at[phase, h, :, 1 - me_c],
                    pair_held.at[phase, h],
                    pair_send.at[phase, h],
                    pair_recv.at[phase, h],
                    (sibling, me_z),
                )

        def chip_parts(phase):
            for h in range(heads):
                arrived(pair_held.at[phase, h], pair_recv.at[phase, h])
                chip_part[phase, h] = part[phase, h, :, me_c] + pair_held[phase, h]
                for n, p in enumerate(chip_ids):
                    start(
                        chip_part.at[phase, h, p],
                        part_held.at[phase, me_p, h],
                        part_send.at[phase, h, n],
                        part_recv.at[phase, h, n],
                        (2 * p + me_c, me_z),
                    )
                part_held[phase, me_p, h] = chip_part[phase, h, me_p]

        def tied(phase):
            sums = []
            for h in range(heads):
                for n in range(chips - 1):
                    arrived(part_held.at[phase, n, h], part_recv.at[phase, h, n])
                x = part_held[phase, 0, h]
                for p in range(1, chips):
                    x = x + part_held[phase, p, h]
                sums.append(x)
            return sums

        def send_prob(phase, n, r, device):
            block = prob.at[phase, pl.ds(0, heads), r]
            start(block, block, prob_send.at[phase, n], prob_recv.at[phase, n], (device, me_z))

        def spread_probs(phase, values):
            for h, x in enumerate(values):
                prob[phase, h, me_r] = x.astype(jnp.bfloat16)
            for n, p in enumerate(chip_ids):
                send_prob(phase, n, me_r, 2 * p + me_c)
            send_prob(phase, chips - 1, me_r, sibling)

        def forward_probs(phase):
            for n in range(chips - 1):
                r = 2 * lax.rem(me_p + chips - 1 - n, chips) + me_c
                arrived(prob.at[phase, pl.ds(0, heads), r], prob_recv.at[phase, n])
                send_prob(phase, chips + n, r, sibling)

        def probs(phase):
            for n in range(chips - 1, 2 * chips - 1):
                arrived(prob.at[phase, pl.ds(0, heads), 0], prob_recv.at[phase, n])
            return [prob[phase, h].reshape(total, total) for h in range(heads)]

        def product(array, dot, weights, x, factor):
            y = dot(weights[0], x)
            if end:
                y = jnp.where(first_head(y), y, dot(weights[1], x))
            if factor is not None:
                y = y * factor
            y = y.astype(jnp.bfloat16)
            for s in range(blocks):
                sent_out[array, :, s] = y[:, s * TILE : (s + 1) * TILE].reshape(4, res, TILE)

        def send_out(array, out_ref):
            for n, p in enumerate(partners):
                if end:
                    dst = out_ref.at[:, :, tile_of(z)]
                else:
                    dst = mid_held.at[array, z - 1]
                start(
                    sent_out.at[array, p, pl.ds(0, blocks)],
                    dst,
                    zout_send.at[array, n],
                    zout_recv.at[array, n],
                    (me_r, p),
                )
            if end:
                lo = 0 if z == 0 else 2 * TILE
                out_ref[:, :, lo : lo + TILE] = sent_out[array, z]
            else:
                mid_held[array, z - 1] = sent_out[array, z, : seqs // 2]

        def finish(array, out_ref):
            for n, p in enumerate(partners):
                if is_end(p):
                    arrived(out_ref.at[:, :, tile_of(p)], zout_recv.at[array, n])
                else:
                    arrived(mid_held.at[array, p - 1], zout_recv.at[array, n])
            for s in range(seqs // 2):
                x, y = mid_held[array, 0, s], mid_held[array, 1, s]
                out_ref[2 * s, :, TILE : 2 * TILE] = jnp.concatenate(
                    [x[:, :half], y[:, :half]], axis=-1
                )
                out_ref[2 * s + 1, :, TILE : 2 * TILE] = jnp.concatenate(
                    [x[:, half:], y[:, half:]], axis=-1
                )

        send_in(0, q_ref, True)
        send_in(1, k_ref, True)
        for n in range(2):
            loads[n].wait()
            pack(n, [mid[n, s] for s in range(seqs)])
            send_in(n, None, False)
        loads[2].wait()
        pack(2, [mid[2, s] for s in range(seqs)])
        loads[3].wait()
        loads[4].wait()
        ga = dot_nt(go_ref[...].reshape(seqs * res, go_ref.shape[2]), w_ref[...])
        ga = ga.astype(jnp.bfloat16).reshape(seqs, res, 3 * TILE)
        ga_ref[...] = ga
        if end:
            lo = 0 if z == 0 else 2 * TILE
            held[3, z] = ga[:, :, lo : lo + TILE]
        pack(3, [ga[s, :, TILE : 2 * TILE] for s in range(seqs)])

        while pending:
            pending.pop(0).wait_send()
        send_in(2, v_ref, True)
        send_in(2, None, False)
        send_in(3, ga_ref, True)
        send_in(3, None, False)
        input_of(0)
        input_of(1)
        pair_parts(0, partial_sums(rows_of(0), rows_of(1)))
        chip_parts(0)
        weights = [softmax_rows(x * scale) for x in tied(0)]
        spread_probs(0, weights)
        forward_probs(0)

        input_of(2)
        input_of(3)
        vals, grads = rows_of(2), rows_of(3)
        pair_parts(1, partial_sums(grads, vals))
        w16 = probs(0)
        product(0, dot_nn, w16, vals, None)
        send_out(0, att_ref)
        chip_parts(1)
        product(1, dot_tn, w16, grads, None)
        send_out(1, gv_ref)
        scores = [score_grad(w, g) for w, g in zip(weights, tied(1))]
        spread_probs(1, scores)
        forward_probs(1)
        s16 = probs(1)
        product(2, dot_nn, s16, rows_of(1), scale)
        send_out(2, gq_ref)
        product(3, dot_tn, s16, rows_of(0), scale)
        send_out(3, gk_ref)

        finish(0, att_ref)
        mixed = dot_nn(att_ref[...].reshape(seqs * res, 3 * TILE), w_ref[...])
        mixed_ref[...] = mixed.astype(jnp.bfloat16).reshape(mixed_ref.shape)
        finish(1, gv_ref)
        finish(2, gq_ref)
        finish(3, gk_ref)
        for copy in pending:
            copy.wait_send()

    for z in range(4):
        pl.when(me_z == z)(functools.partial(run, z))


def copy_out(*refs):
    ins, outs, sem = refs[:4], refs[4:8], refs[8]
    copies = [pltpu.make_async_copy(x, y, sem.at[n]) for n, (x, y) in enumerate(zip(ins, outs))]
    for copy in copies:
        copy.start()
    for copy in copies:
        copy.wait()


def fused(rows, queries, keys, values, out_weight, grad_out):
    seqs, res, width = queries.shape
    model_dim = out_weight.shape[1]
    total = 4 * res
    owned = total // rows
    chips = rows // 2
    scale = 1.0 / math.sqrt(width // HEADS * seqs * rows)
    bf16, f32 = jnp.bfloat16, jnp.float32
    dma = pltpu.SemaphoreType.DMA
    hbm = pl.BlockSpec(memory_space=pltpu.HBM)
    vmem = pl.BlockSpec(memory_space=pltpu.VMEM)
    same = jax.ShapeDtypeStruct(queries.shape, bf16)
    shapes = (jax.ShapeDtypeStruct((seqs, res, model_dim), bf16), same, same, same)
    results = pl.pallas_call(
        functools.partial(kernel, rows, scale),
        out_shape=tuple(pltpu.VMEM(x.shape, x.dtype) for x in shapes),
        in_specs=[hbm] * 5,
        out_specs=(vmem,) * 4,
        scratch_shapes=[
            pltpu.VMEM(out_weight.shape, bf16),
            pltpu.VMEM(grad_out.shape, bf16),
            pltpu.VMEM((3, seqs, res, TILE), bf16),
            pltpu.VMEM((seqs, res, width), bf16),
            pltpu.VMEM((4, 2, seqs // 2, res, TILE), bf16),
            pltpu.VMEM((4, 4, seqs, res, TILE), bf16),
            pltpu.VMEM((2, 2, chips, 2, owned, total), f32),
            pltpu.VMEM((2, 2, chips, owned, total), f32),
            pltpu.VMEM((2, 2, chips, owned, total), f32),
            pltpu.VMEM((2, chips, 2, owned, total), f32),
            pltpu.VMEM((2, 2, rows, owned, total), bf16),
            pltpu.VMEM((4, 4, seqs, res, TILE), bf16),
            pltpu.VMEM((4, 2, seqs // 2, res, TILE), bf16),
            pltpu.VMEM((seqs, res, width), bf16),
            dma((8,)),
            dma((4, 3)),
            dma((4, 3)),
            dma((2, 2)),
            dma((2, 2)),
            dma((2, 2, chips - 1)),
            dma((2, 2, chips - 1)),
            dma((2, rows - 1)),
            dma((2, rows - 1)),
            dma((4, 3)),
            dma((4, 3)),
        ],
        compiler_params=pltpu.CompilerParams(
            collective_id=0, has_side_effects=True, vmem_limit_bytes=62 * 1024 * 1024
        ),
    )(queries, keys, values, out_weight, grad_out)
    return pl.pallas_call(
        copy_out,
        out_shape=shapes,
        in_specs=[vmem] * 4,
        out_specs=(pl.BlockSpec(memory_space=pl.ANY),) * 4,
        scratch_shapes=[dma((4,))],
        compiler_params=pltpu.CompilerParams(vmem_limit_bytes=2 * 1024 * 1024),
    )(*results)


def fits(rows, cols, seqs, res, width):
    total = cols * res
    return (
        cols == 4
        and rows > 1
        and rows % 2 == 0
        and seqs == 4
        and width == HEADS * 64
        and res % 16 == 0
        and total % (16 * rows) == 0
        and total <= 512
    )


def solution(mesh):
    placed = (
        P("row", "res", None),
        P("row", "res", None),
        P("row", "res", None),
        P(),
        P("row", "res", None),
    )
    rows, cols = mesh.shape["row"], mesh.shape["res"]

    def body(queries, keys, values, out_weight, grad_out):
        if fits(rows, cols, *queries.shape):
            return fused(rows, queries, keys, values, out_weight, grad_out)
        return on_device(queries, keys, values, out_weight, grad_out)

    return jax.shard_map(
        body,
        mesh=mesh,
        in_specs=placed,
        out_specs=(
            P("row", "res", None),
            P("row", "res", None),
            P("row", "res", None),
            P("row", "res", None),
        ),
        check_vma=False,
    )
```

```python
import functools
import math

import jax
import jax.numpy as jnp
from jax import lax
from jax.experimental import pallas as pl
from jax.experimental.pallas import tpu as pltpu
from jax.sharding import PartitionSpec as P

HEADS = 6
MESH = pl.DeviceIdType.MESH
TILE = 128


def split_heads(array):
    return array.reshape(array.shape[0], array.shape[1], HEADS, array.shape[2] // HEADS)


def softmax_rows(logits):
    top = jnp.max(logits, axis=-1, keepdims=True)
    expo = jnp.exp(logits - top)
    return expo / jnp.sum(expo, axis=-1, keepdims=True)


def score_grad(weights, grads):
    return weights * (grads - jnp.sum(weights * grads, axis=-1, keepdims=True))


def on_device(queries, keys, values, out_weight, grad_out):
    seq_dev, res_dev, width = queries.shape
    model_dim = out_weight.shape[1]
    head_dim = width // HEADS
    total_res = res_dev * lax.axis_size("res")
    logit_scale = 1.0 / math.sqrt(head_dim * seq_dev * lax.axis_size("row"))
    grad_flat = lax.dot_general(
        grad_out.reshape(seq_dev * res_dev, model_dim),
        out_weight,
        (((1,), (1,)), ((), ())),
        preferred_element_type=jnp.float32,
    )
    grad_attended = grad_flat.astype(jnp.bfloat16).reshape(seq_dev, res_dev, width)
    key_all, value_all = (
        lax.all_gather(keys, "res", axis=1, tiled=True),
        lax.all_gather(values, "res", axis=1, tiled=True),
    )
    key_heads = split_heads(key_all)
    value_heads = split_heads(value_all)
    partial_logits = jnp.einsum(
        "sihd,sjhd->hij", split_heads(queries), key_heads, preferred_element_type=jnp.float32
    )
    partial_logits = partial_logits.reshape(HEADS * res_dev, total_res)
    tied_sum = lax.psum(partial_logits, "row") * logit_scale
    full_weights = softmax_rows(tied_sum)
    weights16 = full_weights.astype(jnp.bfloat16)
    weights_heads = weights16.reshape(HEADS, res_dev, total_res)
    attended = jnp.einsum(
        "hij,sjhd->sihd", weights_heads, value_heads, preferred_element_type=jnp.float32
    )
    attended = attended.astype(jnp.bfloat16).reshape(seq_dev * res_dev, width)
    mixed_out = jnp.dot(attended, out_weight, preferred_element_type=jnp.float32)
    mixed_out = mixed_out.astype(jnp.bfloat16).reshape(seq_dev, res_dev, model_dim)
    grad_partial = jnp.einsum(
        "sihd,sjhd->hij",
        split_heads(grad_attended),
        value_heads,
        preferred_element_type=jnp.float32,
    )
    grad_partial = grad_partial.reshape(HEADS * res_dev, total_res)
    tied_grads = lax.psum(grad_partial, "row")
    scores16 = score_grad(full_weights, tied_grads).astype(jnp.bfloat16)
    score_heads = scores16.reshape(HEADS, res_dev, total_res)
    grad_query = (
        jnp.einsum("hij,sjhd->sihd", score_heads, key_heads, preferred_element_type=jnp.float32)
        * logit_scale
    )
    grad_query = grad_query.astype(jnp.bfloat16).reshape(seq_dev, res_dev, width)
    query_all, grad_all = (
        lax.all_gather(queries, "res", axis=1, tiled=True),
        lax.all_gather(grad_attended, "res", axis=1, tiled=True),
    )
    weights_cols, scores_cols = (
        lax.all_to_all(weights_heads, "res", split_axis=2, concat_axis=1, tiled=True),
        lax.all_to_all(score_heads, "res", split_axis=2, concat_axis=1, tiled=True),
    )
    grad_value = jnp.einsum(
        "hij,sihd->sjhd", weights_cols, split_heads(grad_all), preferred_element_type=jnp.float32
    )
    grad_value = grad_value.astype(jnp.bfloat16).reshape(seq_dev, res_dev, width)
    grad_key = (
        jnp.einsum(
            "hij,sihd->sjhd",
            scores_cols,
            split_heads(query_all),
            preferred_element_type=jnp.float32,
        )
        * logit_scale
    )
    grad_key = grad_key.astype(jnp.bfloat16).reshape(seq_dev, res_dev, width)
    return (mixed_out, grad_query, grad_key, grad_value)


def dot_nt(a, b):
    return lax.dot_general(a, b, (((1,), (1,)), ((), ())), preferred_element_type=jnp.float32)


def dot_tn(a, b):
    return lax.dot_general(a, b, (((0,), (0,)), ((), ())), preferred_element_type=jnp.float32)


def dot_nn(a, b):
    return jnp.dot(a, b, preferred_element_type=jnp.float32)


def is_end(z):
    return z in (0, 3)


def tile_of(z):
    return pl.ds(0 if z == 0 else 2 * TILE, TILE)


def kernel(
    rows,
    scale,
    q_ref,
    k_ref,
    v_ref,
    w_hbm,
    go_hbm,
    mixed_ref,
    gq_ref,
    gk_ref,
    gv_ref,
    w_ref,
    go_ref,
    mid,
    ga_ref,
    packed,
    held,
    part,
    pair_held,
    chip_part,
    part_held,
    prob,
    sent_out,
    mid_held,
    att_ref,
    load_sem,
    zin_send,
    zin_recv,
    pair_send,
    pair_recv,
    part_send,
    part_recv,
    prob_send,
    prob_recv,
    zout_send,
    zout_recv,
):
    me_r, me_z = lax.axis_index("row"), lax.axis_index("res")
    seqs, res, _ = q_ref.shape
    total = 4 * res
    owned = total // rows
    half = TILE // 2
    chips = rows // 2
    me_c, me_p = lax.rem(me_r, 2), me_r // 2
    sibling = me_r + 1 - 2 * me_c
    chip_ids = [lax.rem(me_p + d, chips) for d in range(1, chips)]
    inputs = (q_ref, k_ref, v_ref)

    barrier = pltpu.get_barrier_semaphore()
    for d in range(1, 4):
        pl.semaphore_signal(
            barrier, inc=1, device_id=(me_r, lax.rem(me_z + d, 4)), device_id_type=MESH
        )
    pl.semaphore_signal(barrier, inc=1, device_id=(sibling, me_z), device_id_type=MESH)
    for p in chip_ids:
        pl.semaphore_signal(barrier, inc=1, device_id=(2 * p + me_c, me_z), device_id_type=MESH)

    loads = [
        pltpu.make_async_copy(x.at[:, :, pl.ds(TILE, TILE)], mid.at[n], load_sem.at[n])
        for n, x in enumerate(inputs)
    ]
    loads.append(pltpu.make_async_copy(w_hbm, w_ref, load_sem.at[3]))
    loads.append(pltpu.make_async_copy(go_hbm, go_ref, load_sem.at[4]))
    for load in loads:
        load.start()
    pl.semaphore_wait(barrier, 4 + len(chip_ids))

    def run(z):
        end = is_end(z)
        heads = 2 if end else 1
        blocks = seqs if end else seqs // 2
        partners = (z ^ 2, z ^ 3, z ^ 1)
        pending = []

        def start(src, dst, send, recv, device):
            copy = pltpu.make_async_remote_copy(
                src_ref=src,
                dst_ref=dst,
                send_sem=send,
                recv_sem=recv,
                device_id=device,
                device_id_type=MESH,
            )
            copy.start()
            pending.append(copy)

        def arrived(ref, sem):
            pltpu.make_async_copy(ref, ref, sem).wait()

        def slots(array, source):
            return held.at[array, source, pl.ds(0, blocks)]

        own = []
        if end:
            for n, x in enumerate(inputs):
                copy = pltpu.make_async_copy(x.at[:, :, tile_of(z)], slots(n, z), load_sem.at[5 + n])
                copy.start()
                own.append(copy)

        def send_in(array, x, to_ends):
            for n, p in enumerate(partners):
                if is_end(p) != to_ends:
                    continue
                if to_ends:
                    src, dst = x.at[:, :, tile_of(p)], held.at[array, z]
                else:
                    src, dst = packed.at[array, p - 1], held.at[array, z, pl.ds(0, seqs // 2)]
                start(src, dst, zin_send.at[array, n], zin_recv.at[array, n], (me_r, p))

        def pack(array, tiles):
            for s in range(seqs // 2):
                x, y = tiles[2 * s], tiles[2 * s + 1]
                packed[array, 0, s] = jnp.concatenate([x[:, :half], y[:, :half]], axis=-1)
                packed[array, 1, s] = jnp.concatenate([x[:, half:], y[:, half:]], axis=-1)
            if not end:
                held[array, z, : seqs // 2] = packed[array, z - 1]

        def input_of(array):
            if end:
                own_wait = own[array] if array < 3 else None
                if own_wait is not None:
                    own_wait.wait()
            for n, p in enumerate(partners):
                arrived(slots(array, p), zin_recv.at[array, n])

        def rows_of(array):
            return jnp.concatenate(
                [held[array, :, s].reshape(total, TILE) for s in range(blocks)], axis=-1
            )

        def first_head(x):
            return lax.rem(lax.broadcasted_iota(jnp.int32, x.shape, 1), TILE) < half

        def partial_sums(a, b):
            if not end:
                return [dot_nt(a, b)]
            first, zero = first_head(a), jnp.zeros_like(a)
            return [dot_nt(jnp.where(first, a, zero), b), dot_nt(jnp.where(first, zero, a), b)]

        def pair_parts(phase, sums):
            for h, x in enumerate(sums):
                part[phase, h] = x.reshape(chips, 2, owned, total)
            start(
                part.at[phase, pl.ds(0, heads), :, 1 - me_c],
                pair_held.at[phase, pl.ds(0, heads)],
                pair_send.at[phase],
                pair_recv.at[phase],
                (sibling, me_z),
            )

        def chip_parts(phase):
            arrived(pair_held.at[phase, pl.ds(0, heads)], pair_recv.at[phase])
            for h in range(heads):
                chip_part[phase, h] = part[phase, h, :, me_c] + pair_held[phase, h]
            for n, p in enumerate(chip_ids):
                start(
                    chip_part.at[phase, pl.ds(0, heads), p],
                    part_held.at[phase, me_p, pl.ds(0, heads)],
                    part_send.at[phase, n],
                    part_recv.at[phase, n],
                    (2 * p + me_c, me_z),
                )
            for h in range(heads):
                part_held[phase, me_p, h] = chip_part[phase, h, me_p]

        def tied(phase):
            for n in range(chips - 1):
                arrived(part_held.at[phase, n, pl.ds(0, heads)], part_recv.at[phase, n])
            sums = []
            for h in range(heads):
                x = part_held[phase, 0, h]
                for p in range(1, chips):
                    x = x + part_held[phase, p, h]
                sums.append(x)
            return sums

        def send_prob(phase, n, r, device):
            block = prob.at[phase, pl.ds(0, heads), r]
            start(block, block, prob_send.at[phase, n], prob_recv.at[phase, n], (device, me_z))

        def spread_probs(phase, values):
            for h, x in enumerate(values):
                prob[phase, h, me_r] = x.astype(jnp.bfloat16)
            for n, p in enumerate(chip_ids):
                send_prob(phase, n, me_r, 2 * p + me_c)
            send_prob(phase, chips - 1, me_r, sibling)

        def forward_probs(phase):
            for n in range(chips - 1):
                r = 2 * lax.rem(me_p + chips - 1 - n, chips) + me_c
                arrived(prob.at[phase, pl.ds(0, heads), r], prob_recv.at[phase, n])
                send_prob(phase, chips + n, r, sibling)

        def probs(phase):
            for n in range(chips - 1, 2 * chips - 1):
                arrived(prob.at[phase, pl.ds(0, heads), 0], prob_recv.at[phase, n])
            return [prob[phase, h].reshape(total, total) for h in range(heads)]

        def product(array, dot, weights, x, factor):
            y = dot(weights[0], x)
            if end:
                y = jnp.where(first_head(y), y, dot(weights[1], x))
            if factor is not None:
                y = y * factor
            y = y.astype(jnp.bfloat16)
            for s in range(blocks):
                sent_out[array, :, s] = y[:, s * TILE : (s + 1) * TILE].reshape(4, res, TILE)

        def send_out(array, out_ref, some=range(3)):
            for n in some:
                p = partners[n]
                if end:
                    dst = out_ref.at[:, :, tile_of(z)]
                else:
                    dst = mid_held.at[array, z - 1]
                start(
                    sent_out.at[array, p, pl.ds(0, blocks)],
                    dst,
                    zout_send.at[array, n],
                    zout_recv.at[array, n],
                    (me_r, p),
                )
            if some[0] > 0:
                return
            if end:
                lo = 0 if z == 0 else 2 * TILE
                out_ref[:, :, lo : lo + TILE] = sent_out[array, z]
            else:
                mid_held[array, z - 1] = sent_out[array, z, : seqs // 2]

        def finish(array, out_ref):
            for n, p in enumerate(partners):
                if is_end(p):
                    arrived(out_ref.at[:, :, tile_of(p)], zout_recv.at[array, n])
                else:
                    arrived(mid_held.at[array, p - 1], zout_recv.at[array, n])
            for s in range(seqs // 2):
                x, y = mid_held[array, 0, s], mid_held[array, 1, s]
                out_ref[2 * s, :, TILE : 2 * TILE] = jnp.concatenate(
                    [x[:, :half], y[:, :half]], axis=-1
                )
                out_ref[2 * s + 1, :, TILE : 2 * TILE] = jnp.concatenate(
                    [x[:, half:], y[:, half:]], axis=-1
                )

        send_in(0, q_ref, True)
        send_in(1, k_ref, True)
        for n in range(2):
            loads[n].wait()
            pack(n, [mid[n, s] for s in range(seqs)])
            send_in(n, None, False)
        loads[2].wait()
        pack(2, [mid[2, s] for s in range(seqs)])
        loads[3].wait()
        loads[4].wait()
        ga = dot_nt(go_ref[...].reshape(seqs * res, go_ref.shape[2]), w_ref[...])
        ga = ga.astype(jnp.bfloat16).reshape(seqs, res, 3 * TILE)
        ga_ref[...] = ga
        if end:
            lo = 0 if z == 0 else 2 * TILE
            held[3, z] = ga[:, :, lo : lo + TILE]
        pack(3, [ga[s, :, TILE : 2 * TILE] for s in range(seqs)])

        while pending:
            pending.pop(0).wait_send()
        send_in(2, v_ref, True)
        input_of(0)
        input_of(1)
        pair_parts(0, partial_sums(rows_of(0), rows_of(1)))
        send_in(2, None, False)
        chip_parts(0)
        send_in(3, ga_ref, True)
        weights = [softmax_rows(x * scale) for x in tied(0)]
        spread_probs(0, weights)
        send_in(3, None, False)
        forward_probs(0)

        input_of(2)
        input_of(3)
        vals, grads = rows_of(2), rows_of(3)
        pair_parts(1, partial_sums(grads, vals))
        w16 = probs(0)
        product(0, dot_nn, w16, vals, None)
        chip_parts(1)
        send_out(0, att_ref)
        product(1, dot_tn, w16, grads, None)
        scores = [score_grad(w, g) for w, g in zip(weights, tied(1))]
        spread_probs(1, scores)
        send_out(1, gv_ref, range(1))
        forward_probs(1)
        send_out(1, gv_ref, range(1, 3))
        s16 = probs(1)
        product(2, dot_nn, s16, rows_of(1), scale)
        send_out(2, gq_ref)
        product(3, dot_tn, s16, rows_of(0), scale)
        send_out(3, gk_ref)

        finish(0, att_ref)
        mixed = dot_nn(att_ref[...].reshape(seqs * res, 3 * TILE), w_ref[...])
        mixed_ref[...] = mixed.astype(jnp.bfloat16).reshape(mixed_ref.shape)
        finish(1, gv_ref)
        finish(2, gq_ref)
        finish(3, gk_ref)
        for copy in pending:
            copy.wait_send()

    for z in range(4):
        pl.when(me_z == z)(functools.partial(run, z))


def copy_out(*refs):
    ins, outs, sem = refs[:4], refs[4:8], refs[8]
    copies = [pltpu.make_async_copy(x, y, sem.at[n]) for n, (x, y) in enumerate(zip(ins, outs))]
    for copy in copies:
        copy.start()
    for copy in copies:
        copy.wait()


def fused(rows, queries, keys, values, out_weight, grad_out):
    seqs, res, width = queries.shape
    model_dim = out_weight.shape[1]
    total = 4 * res
    owned = total // rows
    chips = rows // 2
    scale = 1.0 / math.sqrt(width // HEADS * seqs * rows)
    bf16, f32 = jnp.bfloat16, jnp.float32
    dma = pltpu.SemaphoreType.DMA
    hbm = pl.BlockSpec(memory_space=pltpu.HBM)
    vmem = pl.BlockSpec(memory_space=pltpu.VMEM)
    same = jax.ShapeDtypeStruct(queries.shape, bf16)
    shapes = (jax.ShapeDtypeStruct((seqs, res, model_dim), bf16), same, same, same)
    results = pl.pallas_call(
        functools.partial(kernel, rows, scale),
        out_shape=tuple(pltpu.VMEM(x.shape, x.dtype) for x in shapes),
        in_specs=[hbm] * 5,
        out_specs=(vmem,) * 4,
        scratch_shapes=[
            pltpu.VMEM(out_weight.shape, bf16),
            pltpu.VMEM(grad_out.shape, bf16),
            pltpu.VMEM((3, seqs, res, TILE), bf16),
            pltpu.VMEM((seqs, res, width), bf16),
            pltpu.VMEM((4, 2, seqs // 2, res, TILE), bf16),
            pltpu.VMEM((4, 4, seqs, res, TILE), bf16),
            pltpu.VMEM((2, 2, chips, 2, owned, total), f32),
            pltpu.VMEM((2, 2, chips, owned, total), f32),
            pltpu.VMEM((2, 2, chips, owned, total), f32),
            pltpu.VMEM((2, chips, 2, owned, total), f32),
            pltpu.VMEM((2, 2, rows, owned, total), bf16),
            pltpu.VMEM((4, 4, seqs, res, TILE), bf16),
            pltpu.VMEM((4, 2, seqs // 2, res, TILE), bf16),
            pltpu.VMEM((seqs, res, width), bf16),
            dma((8,)),
            dma((4, 3)),
            dma((4, 3)),
            dma((2,)),
            dma((2,)),
            dma((2, chips - 1)),
            dma((2, chips - 1)),
            dma((2, rows - 1)),
            dma((2, rows - 1)),
            dma((4, 3)),
            dma((4, 3)),
        ],
        compiler_params=pltpu.CompilerParams(
            collective_id=0, has_side_effects=True, vmem_limit_bytes=62 * 1024 * 1024
        ),
    )(queries, keys, values, out_weight, grad_out)
    return pl.pallas_call(
        copy_out,
        out_shape=shapes,
        in_specs=[vmem] * 4,
        out_specs=(pl.BlockSpec(memory_space=pl.ANY),) * 4,
        scratch_shapes=[dma((4,))],
        compiler_params=pltpu.CompilerParams(vmem_limit_bytes=2 * 1024 * 1024),
    )(*results)


def fits(rows, cols, seqs, res, width):
    total = cols * res
    return (
        cols == 4
        and rows > 1
        and rows % 2 == 0
        and seqs == 4
        and width == HEADS * 64
        and res % 16 == 0
        and total % (16 * rows) == 0
        and total <= 512
    )


def solution(mesh):
    placed = (
        P("row", "res", None),
        P("row", "res", None),
        P("row", "res", None),
        P(),
        P("row", "res", None),
    )
    rows, cols = mesh.shape["row"], mesh.shape["res"]

    def body(queries, keys, values, out_weight, grad_out):
        if fits(rows, cols, *queries.shape):
            return fused(rows, queries, keys, values, out_weight, grad_out)
        return on_device(queries, keys, values, out_weight, grad_out)

    return jax.shard_map(
        body,
        mesh=mesh,
        in_specs=placed,
        out_specs=(
            P("row", "res", None),
            P("row", "res", None),
            P("row", "res", None),
            P("row", "res", None),
        ),
        check_vma=False,
    )
```

```python
import functools
import math

import jax
import jax.numpy as jnp
from jax import lax
from jax.experimental import pallas as pl
from jax.experimental.pallas import tpu as pltpu
from jax.sharding import PartitionSpec as P

HEADS = 6
MESH = pl.DeviceIdType.MESH
TILE = 128


def split_heads(array):
    return array.reshape(array.shape[0], array.shape[1], HEADS, array.shape[2] // HEADS)


def softmax_rows(logits):
    top = jnp.max(logits, axis=-1, keepdims=True)
    expo = jnp.exp(logits - top)
    return expo / jnp.sum(expo, axis=-1, keepdims=True)


def score_grad(weights, grads):
    return weights * (grads - jnp.sum(weights * grads, axis=-1, keepdims=True))


def on_device(queries, keys, values, out_weight, grad_out):
    seq_dev, res_dev, width = queries.shape
    model_dim = out_weight.shape[1]
    head_dim = width // HEADS
    total_res = res_dev * lax.axis_size("res")
    logit_scale = 1.0 / math.sqrt(head_dim * seq_dev * lax.axis_size("row"))
    grad_flat = lax.dot_general(
        grad_out.reshape(seq_dev * res_dev, model_dim),
        out_weight,
        (((1,), (1,)), ((), ())),
        preferred_element_type=jnp.float32,
    )
    grad_attended = grad_flat.astype(jnp.bfloat16).reshape(seq_dev, res_dev, width)
    key_all, value_all = (
        lax.all_gather(keys, "res", axis=1, tiled=True),
        lax.all_gather(values, "res", axis=1, tiled=True),
    )
    key_heads = split_heads(key_all)
    value_heads = split_heads(value_all)
    partial_logits = jnp.einsum(
        "sihd,sjhd->hij", split_heads(queries), key_heads, preferred_element_type=jnp.float32
    )
    partial_logits = partial_logits.reshape(HEADS * res_dev, total_res)
    tied_sum = lax.psum(partial_logits, "row") * logit_scale
    full_weights = softmax_rows(tied_sum)
    weights16 = full_weights.astype(jnp.bfloat16)
    weights_heads = weights16.reshape(HEADS, res_dev, total_res)
    attended = jnp.einsum(
        "hij,sjhd->sihd", weights_heads, value_heads, preferred_element_type=jnp.float32
    )
    attended = attended.astype(jnp.bfloat16).reshape(seq_dev * res_dev, width)
    mixed_out = jnp.dot(attended, out_weight, preferred_element_type=jnp.float32)
    mixed_out = mixed_out.astype(jnp.bfloat16).reshape(seq_dev, res_dev, model_dim)
    grad_partial = jnp.einsum(
        "sihd,sjhd->hij",
        split_heads(grad_attended),
        value_heads,
        preferred_element_type=jnp.float32,
    )
    grad_partial = grad_partial.reshape(HEADS * res_dev, total_res)
    tied_grads = lax.psum(grad_partial, "row")
    scores16 = score_grad(full_weights, tied_grads).astype(jnp.bfloat16)
    score_heads = scores16.reshape(HEADS, res_dev, total_res)
    grad_query = (
        jnp.einsum("hij,sjhd->sihd", score_heads, key_heads, preferred_element_type=jnp.float32)
        * logit_scale
    )
    grad_query = grad_query.astype(jnp.bfloat16).reshape(seq_dev, res_dev, width)
    query_all, grad_all = (
        lax.all_gather(queries, "res", axis=1, tiled=True),
        lax.all_gather(grad_attended, "res", axis=1, tiled=True),
    )
    weights_cols, scores_cols = (
        lax.all_to_all(weights_heads, "res", split_axis=2, concat_axis=1, tiled=True),
        lax.all_to_all(score_heads, "res", split_axis=2, concat_axis=1, tiled=True),
    )
    grad_value = jnp.einsum(
        "hij,sihd->sjhd", weights_cols, split_heads(grad_all), preferred_element_type=jnp.float32
    )
    grad_value = grad_value.astype(jnp.bfloat16).reshape(seq_dev, res_dev, width)
    grad_key = (
        jnp.einsum(
            "hij,sihd->sjhd",
            scores_cols,
            split_heads(query_all),
            preferred_element_type=jnp.float32,
        )
        * logit_scale
    )
    grad_key = grad_key.astype(jnp.bfloat16).reshape(seq_dev, res_dev, width)
    return (mixed_out, grad_query, grad_key, grad_value)


def dot_nt(a, b):
    return lax.dot_general(a, b, (((1,), (1,)), ((), ())), preferred_element_type=jnp.float32)


def dot_tn(a, b):
    return lax.dot_general(a, b, (((0,), (0,)), ((), ())), preferred_element_type=jnp.float32)


def dot_nn(a, b):
    return jnp.dot(a, b, preferred_element_type=jnp.float32)


def is_end(z):
    return z in (0, 3)


def tile_of(z):
    return pl.ds(0 if z == 0 else 2 * TILE, TILE)


def kernel(
    rows,
    scale,
    q_ref,
    k_ref,
    v_ref,
    w_hbm,
    go_hbm,
    mixed_ref,
    gq_ref,
    gk_ref,
    gv_ref,
    w_ref,
    go_ref,
    mid,
    ga_ref,
    packed,
    held,
    part,
    pair_held,
    chip_part,
    part_held,
    prob,
    sent_out,
    mid_held,
    att_ref,
    load_sem,
    zin_send,
    zin_recv,
    pair_send,
    pair_recv,
    part_send,
    part_recv,
    prob_send,
    prob_recv,
    zout_send,
    zout_recv,
):
    me_r, me_z = lax.axis_index("row"), lax.axis_index("res")
    seqs, res, _ = q_ref.shape
    total = 4 * res
    owned = total // rows
    half = TILE // 2
    chips = rows // 2
    me_c, me_p = lax.rem(me_r, 2), me_r // 2
    sibling = me_r + 1 - 2 * me_c
    chip_ids = [lax.rem(me_p + d, chips) for d in range(1, chips)]
    inputs = (q_ref, k_ref, v_ref)

    barrier = pltpu.get_barrier_semaphore()
    for d in range(1, 4):
        pl.semaphore_signal(
            barrier, inc=1, device_id=(me_r, lax.rem(me_z + d, 4)), device_id_type=MESH
        )
    pl.semaphore_signal(barrier, inc=1, device_id=(sibling, me_z), device_id_type=MESH)
    for p in chip_ids:
        pl.semaphore_signal(barrier, inc=1, device_id=(2 * p + me_c, me_z), device_id_type=MESH)

    loads = [
        pltpu.make_async_copy(x.at[:, :, pl.ds(TILE, TILE)], mid.at[n], load_sem.at[n])
        for n, x in enumerate(inputs)
    ]
    loads.append(pltpu.make_async_copy(w_hbm, w_ref, load_sem.at[3]))
    loads.append(pltpu.make_async_copy(go_hbm, go_ref, load_sem.at[4]))
    for load in loads:
        load.start()
    pl.semaphore_wait(barrier, 4 + len(chip_ids))

    def run(z):
        end = is_end(z)
        heads = 2 if end else 1
        blocks = seqs if end else seqs // 2
        partners = (z ^ 2, z ^ 3, z ^ 1)
        pending = []

        def start(src, dst, send, recv, device):
            copy = pltpu.make_async_remote_copy(
                src_ref=src,
                dst_ref=dst,
                send_sem=send,
                recv_sem=recv,
                device_id=device,
                device_id_type=MESH,
            )
            copy.start()
            pending.append(copy)

        def arrived(ref, sem):
            pltpu.make_async_copy(ref, ref, sem).wait()

        def slots(array, source):
            return held.at[array, source, pl.ds(0, blocks)]

        own = []
        if end:
            for n, x in enumerate(inputs):
                copy = pltpu.make_async_copy(x.at[:, :, tile_of(z)], slots(n, z), load_sem.at[5 + n])
                copy.start()
                own.append(copy)

        def send_in(array, x, to_ends):
            for n, p in enumerate(partners):
                if is_end(p) != to_ends:
                    continue
                if to_ends:
                    src, dst = x.at[:, :, tile_of(p)], held.at[array, z]
                else:
                    src, dst = packed.at[array, p - 1], held.at[array, z, pl.ds(0, seqs // 2)]
                start(src, dst, zin_send.at[array, n], zin_recv.at[array, n], (me_r, p))

        def pack(array, tiles):
            for s in range(seqs // 2):
                x, y = tiles[2 * s], tiles[2 * s + 1]
                packed[array, 0, s] = jnp.concatenate([x[:, :half], y[:, :half]], axis=-1)
                packed[array, 1, s] = jnp.concatenate([x[:, half:], y[:, half:]], axis=-1)
            if not end:
                held[array, z, : seqs // 2] = packed[array, z - 1]

        def input_of(array):
            if end:
                own_wait = own[array] if array < 3 else None
                if own_wait is not None:
                    own_wait.wait()
            for n, p in enumerate(partners):
                arrived(slots(array, p), zin_recv.at[array, n])

        def rows_of(array):
            return jnp.concatenate(
                [held[array, :, s].reshape(total, TILE) for s in range(blocks)], axis=-1
            )

        def first_head(x):
            return lax.rem(lax.broadcasted_iota(jnp.int32, x.shape, 1), TILE) < half

        def partial_sums(a, b):
            if not end:
                return [dot_nt(a, b)]
            first, zero = first_head(a), jnp.zeros_like(a)
            return [dot_nt(jnp.where(first, a, zero), b), dot_nt(jnp.where(first, zero, a), b)]

        def pair_parts(phase, sums):
            for h, x in enumerate(sums):
                part[phase, h] = x.reshape(chips, 2, owned, total)
            start(
                part.at[phase, pl.ds(0, heads), :, 1 - me_c],
                pair_held.at[phase, pl.ds(0, heads)],
                pair_send.at[phase],
                pair_recv.at[phase],
                (sibling, me_z),
            )

        def chip_parts(phase):
            arrived(pair_held.at[phase, pl.ds(0, heads)], pair_recv.at[phase])
            for h in range(heads):
                chip_part[phase, h] = part[phase, h, :, me_c] + pair_held[phase, h]
            for n, p in enumerate(chip_ids):
                start(
                    chip_part.at[phase, pl.ds(0, heads), p],
                    part_held.at[phase, me_p, pl.ds(0, heads)],
                    part_send.at[phase, n],
                    part_recv.at[phase, n],
                    (2 * p + me_c, me_z),
                )
            for h in range(heads):
                part_held[phase, me_p, h] = chip_part[phase, h, me_p]

        def tied(phase):
            for n in range(chips - 1):
                arrived(part_held.at[phase, n, pl.ds(0, heads)], part_recv.at[phase, n])
            sums = []
            for h in range(heads):
                x = part_held[phase, 0, h]
                for p in range(1, chips):
                    x = x + part_held[phase, p, h]
                sums.append(x)
            return sums

        def send_prob(phase, n, r, device):
            block = prob.at[phase, pl.ds(0, heads), r]
            start(block, block, prob_send.at[phase, n], prob_recv.at[phase, n], (device, me_z))

        def spread_probs(phase, values):
            for h, x in enumerate(values):
                prob[phase, h, me_r] = x.astype(jnp.bfloat16)
            for n, p in enumerate(chip_ids):
                send_prob(phase, n, me_r, 2 * p + me_c)
            send_prob(phase, chips - 1, me_r, sibling)

        def forward_probs(phase):
            for n in range(chips - 1):
                r = 2 * lax.rem(me_p + chips - 1 - n, chips) + me_c
                arrived(prob.at[phase, pl.ds(0, heads), r], prob_recv.at[phase, n])
                send_prob(phase, chips + n, r, sibling)

        def probs(phase):
            for n in range(chips - 1, 2 * chips - 1):
                arrived(prob.at[phase, pl.ds(0, heads), 0], prob_recv.at[phase, n])
            return [prob[phase, h].reshape(total, total) for h in range(heads)]

        def product(array, dot, weights, x, factor):
            y = dot(weights[0], x)
            if end:
                y = jnp.where(first_head(y), y, dot(weights[1], x))
            if factor is not None:
                y = y * factor
            y = y.astype(jnp.bfloat16)
            for s in range(blocks):
                sent_out[array, :, s] = y[:, s * TILE : (s + 1) * TILE].reshape(4, res, TILE)

        def send_out(array, out_ref):
            for n, p in enumerate(partners):
                if end:
                    dst = out_ref.at[:, :, tile_of(z)]
                else:
                    dst = mid_held.at[array, z - 1]
                start(
                    sent_out.at[array, p, pl.ds(0, blocks)],
                    dst,
                    zout_send.at[array, n],
                    zout_recv.at[array, n],
                    (me_r, p),
                )
            if end:
                lo = 0 if z == 0 else 2 * TILE
                out_ref[:, :, lo : lo + TILE] = sent_out[array, z]
            else:
                mid_held[array, z - 1] = sent_out[array, z, : seqs // 2]

        def finish(array, out_ref):
            for n, p in enumerate(partners):
                if is_end(p):
                    arrived(out_ref.at[:, :, tile_of(p)], zout_recv.at[array, n])
                else:
                    arrived(mid_held.at[array, p - 1], zout_recv.at[array, n])
            for s in range(seqs // 2):
                x, y = mid_held[array, 0, s], mid_held[array, 1, s]
                out_ref[2 * s, :, TILE : 2 * TILE] = jnp.concatenate(
                    [x[:, :half], y[:, :half]], axis=-1
                )
                out_ref[2 * s + 1, :, TILE : 2 * TILE] = jnp.concatenate(
                    [x[:, half:], y[:, half:]], axis=-1
                )

        send_in(0, q_ref, True)
        send_in(1, k_ref, True)
        for n in range(2):
            loads[n].wait()
            pack(n, [mid[n, s] for s in range(seqs)])
            send_in(n, None, False)
        send_in(2, v_ref, True)
        loads[2].wait()
        pack(2, [mid[2, s] for s in range(seqs)])
        send_in(2, None, False)
        loads[3].wait()
        loads[4].wait()
        ga = dot_nt(go_ref[...].reshape(seqs * res, go_ref.shape[2]), w_ref[...])
        ga = ga.astype(jnp.bfloat16).reshape(seqs, res, 3 * TILE)
        ga_ref[...] = ga
        if end:
            lo = 0 if z == 0 else 2 * TILE
            held[3, z] = ga[:, :, lo : lo + TILE]
        pack(3, [ga[s, :, TILE : 2 * TILE] for s in range(seqs)])

        input_of(0)
        input_of(1)
        pair_parts(0, partial_sums(rows_of(0), rows_of(1)))
        chip_parts(0)
        send_in(3, ga_ref, True)
        send_in(3, None, False)
        weights = [softmax_rows(x * scale) for x in tied(0)]
        spread_probs(0, weights)
        forward_probs(0)

        input_of(2)
        input_of(3)
        vals, grads = rows_of(2), rows_of(3)
        pair_parts(1, partial_sums(grads, vals))
        w16 = probs(0)
        product(0, dot_nn, w16, vals, None)
        send_out(0, att_ref)
        chip_parts(1)
        product(1, dot_tn, w16, grads, None)
        send_out(1, gv_ref)
        scores = [score_grad(w, g) for w, g in zip(weights, tied(1))]
        spread_probs(1, scores)
        forward_probs(1)
        s16 = probs(1)
        product(2, dot_nn, s16, rows_of(1), scale)
        send_out(2, gq_ref)
        product(3, dot_tn, s16, rows_of(0), scale)
        send_out(3, gk_ref)

        finish(0, att_ref)
        mixed = dot_nn(att_ref[...].reshape(seqs * res, 3 * TILE), w_ref[...])
        mixed_ref[...] = mixed.astype(jnp.bfloat16).reshape(mixed_ref.shape)
        finish(1, gv_ref)
        finish(2, gq_ref)
        finish(3, gk_ref)
        for copy in pending:
            copy.wait_send()

    for z in range(4):
        pl.when(me_z == z)(functools.partial(run, z))


def copy_out(*refs):
    ins, outs, sem = refs[:4], refs[4:8], refs[8]
    copies = [pltpu.make_async_copy(x, y, sem.at[n]) for n, (x, y) in enumerate(zip(ins, outs))]
    for copy in copies:
        copy.start()
    for copy in copies:
        copy.wait()


def fused(rows, queries, keys, values, out_weight, grad_out):
    seqs, res, width = queries.shape
    model_dim = out_weight.shape[1]
    total = 4 * res
    owned = total // rows
    chips = rows // 2
    scale = 1.0 / math.sqrt(width // HEADS * seqs * rows)
    bf16, f32 = jnp.bfloat16, jnp.float32
    dma = pltpu.SemaphoreType.DMA
    hbm = pl.BlockSpec(memory_space=pltpu.HBM)
    vmem = pl.BlockSpec(memory_space=pltpu.VMEM)
    same = jax.ShapeDtypeStruct(queries.shape, bf16)
    shapes = (jax.ShapeDtypeStruct((seqs, res, model_dim), bf16), same, same, same)
    results = pl.pallas_call(
        functools.partial(kernel, rows, scale),
        out_shape=tuple(pltpu.VMEM(x.shape, x.dtype) for x in shapes),
        in_specs=[hbm] * 5,
        out_specs=(vmem,) * 4,
        scratch_shapes=[
            pltpu.VMEM(out_weight.shape, bf16),
            pltpu.VMEM(grad_out.shape, bf16),
            pltpu.VMEM((3, seqs, res, TILE), bf16),
            pltpu.VMEM((seqs, res, width), bf16),
            pltpu.VMEM((4, 2, seqs // 2, res, TILE), bf16),
            pltpu.VMEM((4, 4, seqs, res, TILE), bf16),
            pltpu.VMEM((2, 2, chips, 2, owned, total), f32),
            pltpu.VMEM((2, 2, chips, owned, total), f32),
            pltpu.VMEM((2, 2, chips, owned, total), f32),
            pltpu.VMEM((2, chips, 2, owned, total), f32),
            pltpu.VMEM((2, 2, rows, owned, total), bf16),
            pltpu.VMEM((4, 4, seqs, res, TILE), bf16),
            pltpu.VMEM((4, 2, seqs // 2, res, TILE), bf16),
            pltpu.VMEM((seqs, res, width), bf16),
            dma((8,)),
            dma((4, 3)),
            dma((4, 3)),
            dma((2,)),
            dma((2,)),
            dma((2, chips - 1)),
            dma((2, chips - 1)),
            dma((2, rows - 1)),
            dma((2, rows - 1)),
            dma((4, 3)),
            dma((4, 3)),
        ],
        compiler_params=pltpu.CompilerParams(
            collective_id=0, has_side_effects=True, vmem_limit_bytes=62 * 1024 * 1024
        ),
    )(queries, keys, values, out_weight, grad_out)
    return pl.pallas_call(
        copy_out,
        out_shape=shapes,
        in_specs=[vmem] * 4,
        out_specs=(pl.BlockSpec(memory_space=pl.ANY),) * 4,
        scratch_shapes=[dma((4,))],
        compiler_params=pltpu.CompilerParams(vmem_limit_bytes=2 * 1024 * 1024),
    )(*results)


def fits(rows, cols, seqs, res, width):
    total = cols * res
    return (
        cols == 4
        and rows > 1
        and rows % 2 == 0
        and seqs == 4
        and width == HEADS * 64
        and res % 16 == 0
        and total % (16 * rows) == 0
        and total <= 512
    )


def solution(mesh):
    placed = (
        P("row", "res", None),
        P("row", "res", None),
        P("row", "res", None),
        P(),
        P("row", "res", None),
    )
    rows, cols = mesh.shape["row"], mesh.shape["res"]

    def body(queries, keys, values, out_weight, grad_out):
        if fits(rows, cols, *queries.shape):
            return fused(rows, queries, keys, values, out_weight, grad_out)
        return on_device(queries, keys, values, out_weight, grad_out)

    return jax.shard_map(
        body,
        mesh=mesh,
        in_specs=placed,
        out_specs=(
            P("row", "res", None),
            P("row", "res", None),
            P("row", "res", None),
            P("row", "res", None),
        ),
        check_vma=False,
    )
```
